32 devices in a mesh: row: 4 (over y, core), col: 8 (over z, x).
Axes of the slice: x: 2, y: 2, z: 4, core: 2. Of those that a mesh axis runs over, the one named last changes fastest.
Arguments:
- matrix_tiles: float32 [4, 32, 4, 256, 256], P('row', 'col'), as said below
- tile_rows: int32 [4, 32, 4], P('row', 'col'), may hold values from 0 to 7, as said below
- keep_rows: int32 [4, 32, 4], P('row', 'col'), may hold values from 0 to 7, as said below
- owners: int32 [4, 128, 1], P('row', 'col'), may hold values from 0 to 3; in each aligned block of 16 rows (0 to 15, 16 to 31, ..., all dimensions but the last counted through in order) at most 8 rows name the same one
Outputs:
- owned: float32 [4, 8, 32, 256, 256], P('row', 'col')
The draws below stay inside these ranges and needn't reach their ends.
Inputs may be any that keep to these rules, and one draw needn't show every extreme that they name: `matrix_tiles`: every entry is positive. `tile_rows`: for each r and tile column j the 4 entries are distinct, and include j % 8 where j // 8 == r. `keep_rows`: for each r and tile column j the 4 entries are distinct, and include j % 8 where j // 8 == r. `owners`: among the 16 kept tiles of one row block and one column block, at most 8 go to the same owner.
All inputs are finite; a program needn't handle non-finite values.
Results may differ from the reference program's by a relative error of at most 0.000071.
Values sent between devices are 32-bit elements; how exact they have to be, the bound alone decides.
No kernel may reach another device: no remote copies, remote signals or barrier semaphores. Data moves between devices by JAX's collectives and lax.ppermute only.
A program may use at most 256 MiB of HBM per device.

```python
import math
import jax
import jax.numpy as jnp
import numpy as np
from jax import lax

TILE = 256
TR = 8
NZ = 4
KEEP = 4
NT = 32
CT = 4
MOST = 8
NORD = 8192
N_ROW = 4
N_COL = 8


def distinct_rows(key, count):
    scores = jax.random.randint(key, (N_ROW, NT, TR), 0, 1 << 20) * TR + jnp.arange(TR, dtype=jnp.int32)
    block_index = jnp.arange(N_ROW, dtype=jnp.int32)[:, None, None]
    column_index = jnp.arange(NT, dtype=jnp.int32)[None, :, None]
    level_index = jnp.arange(TR, dtype=jnp.int32)[None, None, :]
    diagonal = (column_index // TR == block_index) & (column_index % TR == level_index)
    scores = jnp.where(diagonal, -1, scores)
    return jnp.argsort(scores, axis=-1)[..., :count].astype(jnp.int32)


def draw_tile_rows(key, part):
    return distinct_rows(jax.random.fold_in(key, 11), NZ)


def draw_keep_rows(key, part):
    return distinct_rows(jax.random.fold_in(key, 13), KEEP)


def draw_matrix_tiles(key, part):
    shape = (N_ROW, NT, NZ, TILE, TILE)
    first = jax.random.fold_in(jax.random.fold_in(key, 17), 0)
    values = jax.random.uniform(first, shape, jnp.float32, 0.2, 1.8)
    return (values * (1.0 / TILE)).astype(jnp.float32)


def assign_block(rng, own, number, rows, number_of, top, bound, slope):
    sequence = jax.random.permutation(rng, number_of)
    packed, ordinary = load_shares(number_of, rows * top, bound, slope, True), load_shares(number_of, rows * top, bound, slope, False)
    places = jnp.arange(number_of)

    def named(sizes, rotation):
        used = int((sizes > 0).sum())
        fixed = max(1, used // 4)
        passed = fixed + (places - fixed + rotation * (used - fixed)) % max(1, number_of - fixed)
        return jnp.zeros((number_of,), jnp.int32).at[sequence[jnp.where(places < fixed, places, passed)]].set(jnp.asarray(sizes, jnp.int32))

    sizes = jnp.where(number % 4 == 0, named(packed, number // 4), named(ordinary, number - number // 4 - 1))
    mixed = jax.random.permutation(jax.random.fold_in(own, 3), number_of)
    giver, sink = mixed[0:number_of // 2 * 2:2], mixed[1:number_of // 2 * 2:2]
    slack = jnp.minimum(sizes[giver] - 1, bound - sizes[sink]) // 2
    slack = jnp.where((giver == sequence[0]) | (sink == sequence[0]) | (sizes[sink] == 0), 0, jnp.maximum(slack, 0))
    passed = jax.random.randint(jax.random.fold_in(own, 4), (number_of // 2,), 0, 1 << 20) % (slack + 1)
    sizes = sizes.at[giver].add(-passed).at[sink].add(passed)
    items = jnp.searchsorted(jnp.cumsum(sizes), jnp.arange(rows * top), side="right").astype(jnp.int32)
    table = items.reshape(top, rows).T
    table = table[jax.random.permutation(jax.random.fold_in(own, 1), rows)]
    rotation = jax.random.randint(jax.random.fold_in(own, 2), (rows, 1), 0, top)
    return jnp.take_along_axis(table, (jnp.arange(top)[None, :] + rotation) % top, axis=1)


def load_shares(count, total, bound, skew, full):
    loads = [(1 << 20) // math.isqrt(rank ** skew) + 1 for rank in range(1, count + 1)]
    largest = bound if full else min(bound, max(-(-total // count), total * loads[0] // sum(loads)))
    least = 1 if total - largest >= count - 1 else 0
    given, spare = [largest] + [least] * (count - 1), total - largest - least * (count - 1)
    while spare > 0:
        candidates = [i for i in range(1, count) if given[i] < largest] or [i for i in range(1, count) if given[i] < bound]
        mass, left = sum([loads[i] for i in candidates]), spare
        for i in candidates:
            addition = min(bound - given[i], max(1, left * loads[i] // mass), spare)
            given[i] = given[i] + addition
            spare = spare - addition
    return np.array(given)


def setup_inputs(seed: int = 0) -> dict:
    streams_of = jax.random.split(jax.random.key(seed), 5)
    matrix_tiles = draw_matrix_tiles(jax.random.fold_in(streams_of[4], 71), 0)
    tile_rows = draw_tile_rows(jax.random.fold_in(streams_of[4], 71), 0)
    keep_rows = draw_keep_rows(jax.random.fold_in(streams_of[4], 71), 0)
    owners_keys = jax.random.split(jax.random.fold_in(streams_of[3], 1), N_ROW * (NT * KEEP) // (CT * KEEP))
    owners_turns = jax.random.permutation(jax.random.fold_in(streams_of[3], 3), N_ROW * (NT * KEEP) // (CT * KEEP))
    owners = jax.vmap(lambda own, number: assign_block(jax.random.fold_in(streams_of[3], 2), own, number, CT * KEEP, N_ROW, 1, MOST, 2))(owners_keys, owners_turns).reshape((N_ROW, NT * KEEP, 1))
    return {"matrix_tiles": matrix_tiles, "tile_rows": tile_rows, "keep_rows": keep_rows, "owners": owners}


def reference(matrix_tiles, tile_rows, keep_rows, owners):
    highest = lax.Precision.HIGHEST
    levels = jnp.arange(TR, dtype=jnp.int32)
    selector = (tile_rows[..., None] == levels).astype(jnp.float32)
    dense = jnp.einsum("rjzl,rjzab->rlajb", selector, matrix_tiles.astype(jnp.float32), precision=highest)
    dense = dense.reshape(NORD, NORD)
    expanded = jnp.dot(dense, dense, precision=highest, preferred_element_type=jnp.float32)
    grid = expanded.reshape(NT, TILE, NT, TILE)
    global_rows = jnp.arange(N_ROW, dtype=jnp.int32)[:, None, None] * TR + keep_rows.astype(jnp.int32)
    columns = jnp.arange(NT, dtype=jnp.int32)[None, :, None]
    kept = grid[global_rows, :, columns, :]
    inflated = kept * kept
    column_total = jnp.sum(inflated, axis=(0, 2, 3))
    normalized = NORD * inflated / column_total[None, :, None, None, :]
    items = CT * KEEP
    values = normalized.reshape(N_ROW, N_COL, items, TILE, TILE)
    targets = owners.reshape(N_ROW, N_COL, items).astype(jnp.int32)
    order = jnp.arange(items, dtype=jnp.int32)
    earlier = jnp.sum(((targets[..., None, :] == targets[..., :, None]) & (order[None, :] < order[:, None])).astype(jnp.int32), axis=-1)
    dest_hit = (targets[..., None] == jnp.arange(N_ROW, dtype=jnp.int32))[..., None]
    slot_hit = (earlier[..., None] == jnp.arange(MOST, dtype=jnp.int32))[..., None, :]
    placing = (dest_hit & slot_hit).astype(jnp.float32)
    owned = jnp.einsum("rcfdn,rcfab->dcrnab", placing, values, precision=highest)
    return owned.reshape(N_ROW, N_COL, N_ROW * MOST, TILE, TILE)
```

```python
import functools

import jax
import jax.numpy as jnp
from jax import lax
from jax.experimental import pallas as pl
from jax.experimental.pallas import tpu as pltpu
from jax.sharding import PartitionSpec as P

TR = 8
CHUNKS = (64, 64, 64, 32, 32)
VMEM = 56 * 1024 * 1024


def split(x):
    high = x.astype(jnp.bfloat16)
    low = (x - high.astype(jnp.float32)).astype(jnp.bfloat16)
    return high, low


def place_kernel(x_ref, *refs):
    o_ref = refs[-1]
    for z in range(x_ref.shape[1]):
        high, low = split(x_ref[0, z])
        o_ref[0, 0, 0, z, 0] = high
        o_ref[0, 0, 0, z, 1] = low


def place(x, buffer, group, relative):
    blocks, count, width = x.shape[0], x.shape[1], x.shape[2]
    out = jax.ShapeDtypeStruct((2, blocks, 4, count, 2, width, width), jnp.bfloat16)
    in_specs = [pl.BlockSpec((1, count, width, width), lambda j: (j, 0, 0, 0))]
    args = [x]
    aliases = {}
    if buffer is not None:
        in_specs.append(pl.BlockSpec(memory_space=pl.ANY))
        args.append(buffer)
        aliases = {1: 0}
    return pl.pallas_call(
        place_kernel,
        grid=(blocks,),
        out_shape=out,
        in_specs=in_specs,
        out_specs=pl.BlockSpec(
            (1, 1, 1, count, 2, width, width),
            lambda j: (group, j, relative, 0, 0, 0, 0),
        ),
        input_output_aliases=aliases,
        compiler_params=pltpu.CompilerParams(vmem_limit_bytes=VMEM),
        cost_estimate=pl.CostEstimate(flops=x.size, bytes_accessed=8 * x.size, transcendentals=0),
        name="place",
    )(*args)


def product_kernel(line, columns, me_ref, meta_ref, b_ref, *refs):
    parts = 2 * line - 1
    a_refs = refs[:parts]
    other_ref, own_ref, raw, halves, total, sems = refs[parts:]
    group, j = pl.program_id(0), pl.program_id(1)
    blocks, count, rows, width = a_refs[0].shape
    record = 3 * blocks * count
    r, c = me_ref[0], me_ref[1]
    q, p = c // 2, c % 2

    def base(rr, cc):
        return (rr * columns + cc) * record

    @pl.when((group == 0) & (j == 0))
    def _():
        def each(act):
            for i in range(parts):
                at = q + i - (line - 1)

                @pl.when((at >= 0) & (at < line))
                def _():
                    act(pltpu.make_async_copy(a_refs[i], raw.at[at], sems.at[i]))

        each(lambda copy: copy.start())
        each(lambda copy: copy.wait())

        def convert(i, _):
            for y in range(count):
                high, low = split(raw[i // blocks, i % blocks, y])
                halves[i, y * rows : (y + 1) * rows, 0:width] = high
                halves[i, y * rows : (y + 1) * rows, width : 2 * width] = low
            return 0

        lax.fori_loop(0, line * blocks, convert, 0)

    total[...] = jnp.zeros_like(total)
    target = jnp.where(group == 0, c + 1 - 2 * p, c)

    def step(t, _):
        rr = jnp.bitwise_xor(r, t // count)
        k = rr * TR + meta_ref[base(rr, target) + j * count + t % count]
        ck = k // blocks

        @pl.when(ck % 2 == p)
        def _():
            kk = k % blocks
            at = (ck // 2) * blocks + kk
            high = halves[at, :, 0:width]
            both = halves[at]
            b_high = b_ref[0, 0, t // count, t % count, 0]
            b_low = b_ref[0, 0, t // count, t % count, 1]
            product = jnp.dot(
                jnp.concatenate([both, high], axis=1),
                jnp.concatenate([b_high, b_high, b_low], axis=0),
                preferred_element_type=jnp.float32,
            )
            levels = base(r, ck) + kk * count
            for y in range(count):
                total[meta_ref[levels + y]] += product[y * rows : (y + 1) * rows]

        return 0

    lax.fori_loop(0, 4 * count, step, 0)
    keeps = base(r, target) + blocks * count + j * count

    @pl.when(group == 0)
    def _():
        for m in range(count):
            other_ref[0, m] = total[meta_ref[keeps + m]]

    @pl.when(group == 1)
    def _():
        for m in range(count):
            own_ref[0, m] = total[meta_ref[keeps + m]]


def product(me, meta, panel, parts, line, columns):
    blocks, count, rows, width = parts[0].shape
    out = jax.ShapeDtypeStruct((blocks, count, rows, width), jnp.float32)
    smem = pl.BlockSpec(memory_space=pltpu.SMEM)
    return pl.pallas_call(
        functools.partial(product_kernel, line, columns),
        grid=(2, blocks),
        out_shape=(out, out),
        in_specs=[
            smem,
            smem,
            pl.BlockSpec(
                (1, 1, 4, count, 2, width, width), lambda g, j: (g, j, 0, 0, 0, 0, 0)
            ),
        ]
        + [pl.BlockSpec(memory_space=pl.ANY)] * len(parts),
        out_specs=(
            pl.BlockSpec(
                (1, count, rows, width), lambda g, j: (jnp.where(g == 0, j, blocks - 1), 0, 0, 0)
            ),
            pl.BlockSpec((1, count, rows, width), lambda g, j: (jnp.where(g == 0, 0, j), 0, 0, 0)),
        ),
        scratch_shapes=[
            pltpu.VMEM((line, blocks, count, rows, width), jnp.float32),
            pltpu.VMEM((line * blocks, count * rows, 2 * width), jnp.bfloat16),
            pltpu.VMEM((TR, rows, width), jnp.float32),
            pltpu.SemaphoreType.DMA((len(parts),)),
        ],
        compiler_params=pltpu.CompilerParams(vmem_limit_bytes=VMEM),
        cost_estimate=pl.CostEstimate(
            flops=3 * 2 * 16 * blocks * count * rows * width * width,
            bytes_accessed=2 * panel.size,
            transcendentals=0,
        ),
        name="product",
    )(me, meta, panel, *parts)


def owned_kernel(columns, sizes, scale, me_ref, meta_ref, sums_ref, *refs):
    chunks = len(sizes)
    sources = refs[: 4 * chunks]
    out_ref, slots, whose, in_sems, out_sems = refs[4 * chunks :]
    blocks, count = sources[0].shape[:2]
    items = blocks * count
    most = items // 2
    record = 3 * items
    r, c = me_ref[0], me_ref[1]
    starts = [sum(sizes[:h]) for h in range(chunks)]

    for s in range(4 * most):
        whose[s] = -1
    for relative in range(4):
        rr = jnp.bitwise_xor(r, relative)

        def place_item(f, n, relative=relative, rr=rr):
            mine = meta_ref[(rr * columns + c) * record + 2 * items + f] == r

            @pl.when(mine)
            def _():
                slot = rr * most + n
                whose[slot] = f // count
                for h in range(chunks):
                    pltpu.make_async_copy(
                        sources[4 * h + relative].at[f // count, f % count],
                        slots.at[slot, pl.ds(starts[h], sizes[h])],
                        in_sems.at[slot],
                    ).start()

            return n + mine.astype(jnp.int32)

        lax.fori_loop(0, items, place_item, jnp.int32(0))

    factors = scale / sums_ref[...]

    def finish(s, _):
        j = whose[s]

        @pl.when(j < 0)
        def _():
            slots[s] = jnp.zeros(slots.shape[1:], jnp.float32)

        for jj in range(blocks):

            @pl.when(j == jj)
            def _():
                pltpu.make_async_copy(slots.at[s], slots.at[s], in_sems.at[s]).wait()
                slots[s] = slots[s] * factors[jj : jj + 1]

        pltpu.make_async_copy(slots.at[s], out_ref.at[s], out_sems.at[s]).start()
        return 0

    lax.fori_loop(0, 4 * most, finish, 0)

    def drain(s, _):
        pltpu.make_async_copy(slots.at[s], out_ref.at[s], out_sems.at[s]).wait()
        return 0

    lax.fori_loop(0, 4 * most, drain, 0)


def owned_tiles(me, meta, sums, sources, columns, sizes, scale):
    blocks, count, _, width = sources[0].shape
    most = blocks * count // 2
    smem = pl.BlockSpec(memory_space=pltpu.SMEM)
    return pl.pallas_call(
        functools.partial(owned_kernel, columns, sizes, scale),
        out_shape=jax.ShapeDtypeStruct((4 * most, width, width), jnp.float32),
        in_specs=[smem, smem, pl.BlockSpec(memory_space=pltpu.VMEM)]
        + [pl.BlockSpec(memory_space=pl.ANY)] * len(sources),
        out_specs=pl.BlockSpec(memory_space=pl.ANY),
        scratch_shapes=[
            pltpu.VMEM((4 * most, width, width), jnp.float32),
            pltpu.SMEM((4 * most,), jnp.int32),
            pltpu.SemaphoreType.DMA((4 * most,)),
            pltpu.SemaphoreType.DMA((4 * most,)),
        ],
        compiler_params=pltpu.CompilerParams(vmem_limit_bytes=VMEM),
        cost_estimate=pl.CostEstimate(
            flops=4 * most * width * width,
            bytes_accessed=32 * most * width * width,
            transcendentals=0,
        ),
        name="owned",
    )(me, meta, sums, *sources)


def on_device(columns, matrix_tiles, tile_rows, keep_rows, owners):
    tiles = matrix_tiles[0]
    blocks, count, width = tiles.shape[0], tiles.shape[1], tiles.shape[2]
    line = columns // 2
    r, c = lax.axis_index("row"), lax.axis_index("col")
    me = jnp.stack([r, c]).astype(jnp.int32)

    core = functools.partial(lax.ppermute, axis_name="row", perm=[(i, i ^ 1) for i in range(4)])
    across = functools.partial(lax.ppermute, axis_name="row", perm=[(i, i ^ 2) for i in range(4)])
    pair = functools.partial(
        lax.ppermute, axis_name="col", perm=[(i, i ^ 1) for i in range(columns)]
    )

    def up(x, hop):
        return lax.ppermute(x, "col", [(i, i + 2) for i in range(2 * hop, columns - 2)])

    def down(x, hop):
        return lax.ppermute(x, "col", [(i + 2, i) for i in range(0, columns - 2 - 2 * hop)])

    sizes = tuple(size * width // sum(CHUNKS) for size in CHUNKS)
    starts = [sum(sizes[:h]) for h in range(len(sizes))]

    def gather(h):
        own = tiles[:, :, starts[h] : starts[h] + sizes[h]]
        below, above = [], []
        rising = falling = own
        for hop in range(line - 1):
            rising, falling = up(rising, hop), down(falling, hop)
            below.append(rising)
            above.append(falling)
        return below[::-1] + [own] + above

    mine = jnp.concatenate(
        [tile_rows.reshape(-1), keep_rows.reshape(-1), owners.reshape(-1)]
    )
    meta = lax.all_gather(mine, ("row", "col"), axis=0, tiled=True)

    gathered = [gather(h) for h in range(len(sizes))]

    half = width // 2
    b_pair, b_across = pair(tiles), across(tiles)
    b_diagonal = jnp.concatenate(
        [across(b_pair[:, :, :half]), pair(b_across[:, :, half:])], axis=2
    )
    shards = [
        (tiles, 1, 0),
        (core(tiles), 1, 1),
        (b_pair, 0, 0),
        (b_across, 1, 2),
        (core(b_pair), 0, 1),
        (core(b_across), 1, 3),
        (b_diagonal, 0, 2),
        (core(b_diagonal), 0, 3),
    ]
    panel = None
    for shard, group, relative in shards:
        panel = place(shard, panel, group, relative)

    sums = jnp.zeros((blocks, width), jnp.float32)
    sources = []
    for h in range(len(sizes)):
        other, own = product(me, meta, panel, gathered[h], line, columns)
        kept = own + pair(other)
        inflated = kept * kept
        opposite = across(inflated)
        four = [inflated, core(inflated), opposite, core(opposite)]
        sources += four
        sums = sums + sum(jnp.sum(x, axis=(1, 2)) for x in four)
    scale = float(4 * TR * width)
    owned = owned_tiles(me, meta, sums, sources, columns, sizes, scale)
    return owned[None, None]


def solution(mesh):
    placed = (
        P("row", "col", None, None, None),
        P("row", "col", None),
        P("row", "col", None),
        P("row", "col", None),
    )
    return jax.shard_map(
        functools.partial(on_device, mesh.shape["col"]),
        mesh=mesh,
        in_specs=placed,
        out_specs=P("row", "col", None, None, None),
        check_vma=False,
    )
```

```python
import functools

import jax
import jax.numpy as jnp
from jax import lax
from jax.experimental import pallas as pl
from jax.experimental.pallas import tpu as pltpu
from jax.sharding import PartitionSpec as P

TR = 8
CHUNKS = (128, 64, 32, 32)
ROWS = 64
FIELDS = 8
RING = 16
MODE = 0
VMEM = 56 * 1024 * 1024


def split(x):
    high = x.astype(jnp.bfloat16)
    low = (x - high.astype(jnp.float32)).astype(jnp.bfloat16)
    return high, low


def place_kernel(pieces, *refs):
    o_ref, mark_ref = refs[-2:]
    mark_ref[...] = jnp.zeros_like(mark_ref)
    start = 0
    for x_ref in refs[:pieces]:
        count, rows = x_ref.shape[1:3]
        for z in range(count):
            high, low = split(x_ref[0, z])
            o_ref[0, 0, 0, z, 0, start : start + rows] = high
            o_ref[0, 0, 0, z, 1, start : start + rows] = low
        start += rows


def place(pieces, buffer, group, relative, rows):
    blocks, count, _, width = pieces[0].shape
    out = jax.ShapeDtypeStruct((2, blocks, 4, count, 2, width, width), jnp.bfloat16)
    in_specs = [pl.BlockSpec((1, count, rows, width), lambda j: (j, 0, 0, 0)) for _ in pieces]
    args = list(pieces)
    aliases = {}
    if buffer is not None:
        in_specs.append(pl.BlockSpec(memory_space=pl.ANY))
        args.append(buffer)
        aliases = {len(pieces): 0}
    size = blocks * count * width * width
    return pl.pallas_call(
        functools.partial(place_kernel, len(pieces)),
        grid=(blocks,),
        out_shape=(out, jax.ShapeDtypeStruct((8, 128), jnp.float32)),
        in_specs=in_specs,
        out_specs=(
            pl.BlockSpec(
                (1, 1, 1, count, 2, width, width),
                lambda j: (group, j, relative, 0, 0, 0, 0),
            ),
            pl.BlockSpec((8, 128), lambda j: (0, 0)),
        ),
        input_output_aliases=aliases,
        compiler_params=pltpu.CompilerParams(vmem_limit_bytes=VMEM),
        cost_estimate=pl.CostEstimate(flops=size, bytes_accessed=8 * size, transcendentals=0),
        name="place",
    )(*args)


def plan_kernel(line, blocks, count, me_ref, meta_ref, levels_ref, plan_ref, kept_ref):
    items = blocks * count
    r, c = me_ref[0], me_ref[1]
    q, p = c // 2, c % 2

    def base(relative, group):
        return (relative * 2 + group) * 3 * items

    def write(n, tile, at, levels):
        plan_ref[FIELDS * n] = tile
        plan_ref[FIELDS * n + 1] = at
        for y in range(count):
            plan_ref[FIELDS * n + 2 + y] = levels(y)

    def column(row, n):
        group, j = row // blocks, row % blocks

        def entry(t, n):
            relative = t // count
            rr = jnp.bitwise_xor(r, relative)
            k = rr * TR + meta_ref[base(relative, group) + j * count + t % count]
            ck = k // blocks
            mine = ck % 2 == p
            levels = (ck // 2 - q + line - 1) * items + (k % blocks) * count
            write(
                n,
                row * 4 * count + t,
                (ck // 2) * blocks + k % blocks,
                lambda y: levels_ref[levels + y],
            )
            return n + mine.astype(jnp.int32)

        n = lax.fori_loop(0, 4 * count, entry, n)
        write(n, row * 4 * count, line * blocks, lambda y: jnp.int32(0))
        n = n + n % 2
        kept_ref[FIELDS * row] = n
        for m in range(count):
            kept_ref[FIELDS * row + 1 + m] = meta_ref[base(0, group) + items + j * count + m]
        return n

    lax.fori_loop(0, 2 * blocks, column, jnp.int32(0))


def make_plan(me, meta, levels, line, blocks, count):
    smem = pl.BlockSpec(memory_space=pltpu.SMEM)
    return pl.pallas_call(
        functools.partial(plan_kernel, line, blocks, count),
        out_shape=(
            jax.ShapeDtypeStruct((FIELDS * (2 * blocks * 4 * count + 2),), jnp.int32),
            jax.ShapeDtypeStruct((FIELDS * 2 * blocks,), jnp.int32),
        ),
        in_specs=[smem] * 3,
        out_specs=(smem, smem),
        name="plan",
    )(me, meta, levels)


def product_kernel(line, start, me_ref, plan_ref, kept_ref, b_ref, *refs):
    parts = 2 * line - 1
    a_refs = refs[:parts]
    other_ref, own_ref, raw, halves, total, ring, a_sems, b_sems = refs[parts:]
    group, j = pl.program_id(0), pl.program_id(1)
    blocks, count, rows, width = raw.shape[1:]
    last = 2 * blocks - 1
    row = group * blocks + j
    q = me_ref[1] // 2
    end = kept_ref[FIELDS * last]

    def fetch(n):
        tile = plan_ref[FIELDS * n]
        slot = n % RING
        return pltpu.make_async_copy(b_ref.at[tile], ring.at[slot], b_sems.at[slot])

    @pl.when(row == 0)
    def _():
        def each(act):
            for i in range(parts):
                at = q + i - (line - 1)

                @pl.when((at >= 0) & (at < line))
                def _():
                    rows_of = a_refs[i].at[:, :, start : start + rows]
                    act(pltpu.make_async_copy(rows_of, raw.at[at], a_sems.at[i]))

        each(lambda copy: copy.start())

        def begin(n, _):
            fetch(n).start()
            return 0

        lax.fori_loop(0, jnp.minimum(end, RING), begin, 0)
        halves[line * blocks] = jnp.zeros(halves.shape[1:], halves.dtype)
        each(lambda copy: copy.wait())

        def convert(i, _):
            for y in range(count):
                high, low = split(raw[i // blocks, i % blocks, y])
                halves[i, y * rows : (y + 1) * rows, 0:width] = high
                halves[i, y * rows : (y + 1) * rows, width : 2 * width] = low
            return 0

        lax.fori_loop(0, line * blocks, convert, 0)

    total[...] = jnp.zeros_like(total)
    first = jnp.where(row == 0, 0, kept_ref[FIELDS * jnp.maximum(row - 1, 0)])

    def multiply(n):
        a = halves[plan_ref[FIELDS * n + 1]]
        slot = n % RING
        b_high, b_low = ring[slot, 0], ring[slot, 1]
        if MODE == 0:
            return jnp.dot(
                jnp.concatenate([a, a[:, 0:width]], axis=1),
                jnp.concatenate([b_high, b_high, b_low], axis=0),
                preferred_element_type=jnp.float32,
            )
        if MODE == 1:
            dot = functools.partial(jnp.dot, preferred_element_type=jnp.float32)
            return dot(a[:, :width], b_high) + dot(a[:, width:], b_high) + dot(a[:, :width], b_low)
        bb = jnp.concatenate([b_high, b_high, b_low], axis=0)
        return jnp.concatenate(
            [
                jnp.dot(
                    jnp.concatenate(
                        [a[y * rows : (y + 1) * rows], a[y * rows : (y + 1) * rows, 0:width]], axis=1
                    ),
                    bb,
                    preferred_element_type=jnp.float32,
                )
                for y in range(count)
            ],
            axis=0,
        )

    def step(i, _):
        n = first + 2 * i
        fetch(n).wait()
        fetch(n + 1).wait()
        products = [multiply(n), multiply(n + 1)]
        for e in range(2):
            for y in range(count):
                level = plan_ref[FIELDS * (n + e) + 2 + y]
                total[level] += products[e][y * rows : (y + 1) * rows]

        @pl.when(n + RING < end)
        def _():
            fetch(n + RING).start()
            fetch(n + RING + 1).start()

        return 0

    lax.fori_loop(0, (kept_ref[FIELDS * row] - first) // 2, step, 0)

    @pl.when(group == 0)
    def _():
        for m in range(count):
            other_ref[0, m] = total[kept_ref[FIELDS * row + 1 + m]]

    @pl.when(group == 1)
    def _():
        for m in range(count):
            own_ref[0, m] = total[kept_ref[FIELDS * row + 1 + m]]


def product(me, plan, panel, parts, line, start, rows):
    blocks, count, _, width = parts[0].shape
    out = jax.ShapeDtypeStruct((blocks, count, rows, width), jnp.float32)
    smem = pl.BlockSpec(memory_space=pltpu.SMEM)
    return pl.pallas_call(
        functools.partial(product_kernel, line, start),
        grid=(2, blocks),
        out_shape=(out, out),
        in_specs=[smem] * 3 + [pl.BlockSpec(memory_space=pl.ANY)] * (1 + len(parts)),
        out_specs=(
            pl.BlockSpec(
                (1, count, rows, width), lambda g, j: (jnp.where(g == 0, j, blocks - 1), 0, 0, 0)
            ),
            pl.BlockSpec((1, count, rows, width), lambda g, j: (jnp.where(g == 0, 0, j), 0, 0, 0)),
        ),
        scratch_shapes=[
            pltpu.VMEM((line, blocks, count, rows, width), jnp.float32),
            pltpu.VMEM((line * blocks + 1, count * rows, 2 * width), jnp.bfloat16),
            pltpu.VMEM((TR, rows, width), jnp.float32),
            pltpu.VMEM((RING, 2, width, width), jnp.bfloat16),
            pltpu.SemaphoreType.DMA((len(parts),)),
            pltpu.SemaphoreType.DMA((RING,)),
        ],
        compiler_params=pltpu.CompilerParams(vmem_limit_bytes=VMEM),
        cost_estimate=pl.CostEstimate(
            flops=3 * 2 * 16 * blocks * count * rows * width * width,
            bytes_accessed=panel.size,
            transcendentals=0,
        ),
        name="product",
    )(me, *plan, panel.reshape(-1, 2, width, width), *parts)


def inflate_kernel(own_ref, other_ref, out_ref):
    count, rows = own_ref.shape[1:3]
    partial = jnp.zeros((8, own_ref.shape[3]), jnp.float32)
    for m in range(count):
        kept = own_ref[0, m] + other_ref[0, m]
        inflated = kept * kept
        out_ref[0, m * rows : (m + 1) * rows] = inflated
        for i in range(0, rows, 8):
            partial += inflated[i : i + 8]
    out_ref[0, count * rows :] = partial


def inflate(own, other):
    blocks, count, rows, width = own.shape
    spec = pl.BlockSpec((1, count, rows, width), lambda j: (j, 0, 0, 0))
    return pl.pallas_call(
        inflate_kernel,
        grid=(blocks,),
        out_shape=jax.ShapeDtypeStruct((blocks, count * rows + 8, width), jnp.float32),
        in_specs=[spec, spec],
        out_specs=pl.BlockSpec((1, count * rows + 8, width), lambda j: (j, 0, 0)),
        cost_estimate=pl.CostEstimate(
            flops=3 * own.size, bytes_accessed=12 * own.size, transcendentals=0
        ),
        name="inflate",
    )(own, other)


def owned_kernel(sizes, blocks, count, scale, me_ref, meta_ref, *refs):
    chunks = len(sizes)
    sources = refs[: 4 * chunks]
    out_ref, slots, partial, whose, in_sems, out_sems, sum_sems = refs[4 * chunks :]
    items = blocks * count
    most = items // 2
    r = me_ref[0]
    starts = [sum(sizes[:h]) for h in range(chunks)]

    def partials(act):
        for i in range(4 * chunks):
            rows = pl.ds(count * sizes[i // 4], 8)
            act(pltpu.make_async_copy(sources[i].at[:, rows], partial.at[i], sum_sems.at[i]))

    partials(lambda copy: copy.start())
    for s in range(4 * most):
        whose[s] = -1
    for relative in range(4):
        rr = jnp.bitwise_xor(r, relative)

        def place_item(f, n, relative=relative, rr=rr):
            mine = meta_ref[((relative * 2 + 1) * 3 + 2) * items + f] == r

            @pl.when(mine)
            def _():
                slot = rr * most + n
                whose[slot] = f // count
                for h in range(chunks):
                    pltpu.make_async_copy(
                        sources[4 * h + relative].at[
                            f // count, pl.ds(pl.multiple_of(f % count * sizes[h], 8), sizes[h])
                        ],
                        slots.at[slot, pl.ds(starts[h], sizes[h])],
                        in_sems.at[slot],
                    ).start()

            return n + mine.astype(jnp.int32)

        lax.fori_loop(0, items, place_item, jnp.int32(0))

    partials(lambda copy: copy.wait())
    factors = scale / jnp.sum(jnp.sum(partial[...], axis=0), axis=1)

    def finish(s, _):
        j = whose[s]

        @pl.when(j < 0)
        def _():
            slots[s] = jnp.zeros(slots.shape[1:], jnp.float32)

        for jj in range(blocks):

            @pl.when(j == jj)
            def _():
                pltpu.make_async_copy(slots.at[s], slots.at[s], in_sems.at[s]).wait()
                slots[s] = slots[s] * factors[jj : jj + 1]

        pltpu.make_async_copy(slots.at[s], out_ref.at[s], out_sems.at[s]).start()
        return 0

    lax.fori_loop(0, 4 * most, finish, 0)

    def drain(s, _):
        pltpu.make_async_copy(slots.at[s], out_ref.at[s], out_sems.at[s]).wait()
        return 0

    lax.fori_loop(0, 4 * most, drain, 0)


def owned_tiles(me, meta, sources, sizes, count, scale):
    blocks, _, width = sources[0].shape
    most = blocks * count // 2
    smem = pl.BlockSpec(memory_space=pltpu.SMEM)
    return pl.pallas_call(
        functools.partial(owned_kernel, sizes, blocks, count, scale),
        out_shape=jax.ShapeDtypeStruct((4 * most, width, width), jnp.float32),
        in_specs=[smem, smem]
        + [pl.BlockSpec(memory_space=pl.ANY)] * len(sources),
        out_specs=pl.BlockSpec(memory_space=pl.ANY),
        scratch_shapes=[
            pltpu.VMEM((4 * most, width, width), jnp.float32),
            pltpu.VMEM((len(sources), blocks, 8, width), jnp.float32),
            pltpu.SMEM((4 * most,), jnp.int32),
            pltpu.SemaphoreType.DMA((4 * most,)),
            pltpu.SemaphoreType.DMA((4 * most,)),
            pltpu.SemaphoreType.DMA((len(sources),)),
        ],
        compiler_params=pltpu.CompilerParams(vmem_limit_bytes=VMEM),
        cost_estimate=pl.CostEstimate(
            flops=4 * most * width * width,
            bytes_accessed=32 * most * width * width,
            transcendentals=0,
        ),
        name="owned",
    )(me, meta, *sources)


def on_device(columns, matrix_tiles, tile_rows, keep_rows, owners):
    tiles = matrix_tiles[0]
    blocks, count, width = tiles.shape[0], tiles.shape[1], tiles.shape[2]
    line = columns // 2
    r, c = lax.axis_index("row"), lax.axis_index("col")
    me = jnp.stack([r, c]).astype(jnp.int32)

    core = functools.partial(lax.ppermute, axis_name="row", perm=[(i, i ^ 1) for i in range(4)])
    across = functools.partial(lax.ppermute, axis_name="row", perm=[(i, i ^ 2) for i in range(4)])
    pair = functools.partial(
        lax.ppermute, axis_name="col", perm=[(i, i ^ 1) for i in range(columns)]
    )

    def up(x, hop):
        return lax.ppermute(x, "col", [(i, i + 2) for i in range(2 * hop, columns - 2)])

    def down(x, hop):
        return lax.ppermute(x, "col", [(i + 2, i) for i in range(0, columns - 2 - 2 * hop)])

    def apart(x, hop):
        rising = [(i, i + 2) for i in range(2 * hop, columns - 2)]
        falling = [(i + 2, i) for i in range(0, columns - 2 - 2 * hop)]
        return lax.ppermute(x, "col", rising + falling)

    sizes = tuple(size * width // sum(CHUNKS) for size in CHUNKS)
    starts = [sum(sizes[:h]) for h in range(len(sizes))]

    chunks, half = len(sizes), width // 2
    notes = jnp.stack([tile_rows[0], keep_rows[0], owners.reshape(blocks, count)], axis=2)
    notes = jnp.pad(notes, ((0, 0), (0, 0), (0, 5))).astype(jnp.float32)
    noted = jnp.broadcast_to(notes[..., None], (blocks, count, 8, width))
    own = [tiles[:, :, start : start + size] for start, size in zip(starts, sizes)]
    own[0] = jnp.concatenate([own[0], noted], axis=2)
    rest = tiles[:, :, half:]
    below, above = [[] for _ in sizes], [[] for _ in sizes]

    ticks = {}

    def at(tick, x):
        ticks.setdefault(tick, []).append(x)
        return x

    def after(tick, x):
        others = ticks.get(tick - 1, ())
        return lax.optimization_barrier((x, *others))[0] if others else x

    def send(tick, move, x, *more):
        return at(tick, move(after(tick, x), *more))

    swapped = []

    def swap(tick, x):
        if swapped:
            x = lax.optimization_barrier((x, swapped[-1]))[0]
        swapped.append(send(tick, core, x))
        return swapped[-1]

    base = line - 1
    hops = {}
    for h in range(chunks):
        for hop in range(line - 1):
            if h == 0:
                tick = hop
            else:
                tick = base + hop + (h - 1 if hop else max(h - 2, 0))
            hops.setdefault(tick, []).append((h, hop))

    panel = None
    sources, waiting, landed, flying = [], [], [], []

    def put(tick, pieces, group, relative):
        nonlocal panel
        panel, mark = place(pieces, panel, group, relative, half)
        at(tick, mark)

    tick = 0
    while tick <= max(hops) + 1 or waiting or landed or flying:
        for h, hop in hops.get(tick, ()):
            rising, falling = (below[h][-1], above[h][-1]) if hop else (own[h], own[h])
            if line - 1 - hop < hop:
                both = send(tick, apart, jnp.where(c // 2 >= hop, rising, falling), hop)
                below[h].append(both)
                above[h].append(both)
                continue
            below[h].append(send(tick, up, rising, hop))
            above[h].append(send(tick, down, falling, hop))
        if tick == 0:
            b_pair, b_across = [send(0, pair, own[0])], [send(0, across, own[0])]
            core_own = [swap(0, own[0]), swap(0, rest)]
            put(0, [own[0], rest], 1, 0)
            put(0, core_own, 1, 1)
        if tick == 1:
            b_pair.append(send(1, pair, rest))
            b_across.append(send(1, across, rest))
            core_pair, core_across = [swap(1, b_pair[0])], [swap(1, b_across[0])]
        if tick == 2:
            b_diagonal = [send(2, across, b_pair[0]), send(2, pair, b_across[1])]
            core_pair.append(swap(2, b_pair[1]))
            core_across.append(swap(2, b_across[1]))
            put(2, b_pair, 0, 0)
            put(2, b_across, 1, 2)
            put(2, core_pair, 0, 1)
            put(2, core_across, 1, 3)
        if tick == max(base, 3):
            core_diagonal = [swap(tick, x) for x in b_diagonal]
            put(tick, b_diagonal, 0, 2)
            put(tick, core_diagonal, 0, 3)
            known = [
                x[0][:, :, half : half + 3, 0]
                for x in (
                    b_pair,
                    own,
                    core_pair,
                    core_own,
                    b_diagonal,
                    b_across,
                    core_diagonal,
                    core_across,
                )
            ]
            meta = jnp.transpose(jnp.stack(known), (0, 3, 1, 2)).astype(jnp.int32).reshape(-1)
            levels = jnp.stack(
                [x[:, :, half, 0] for x in below[0][::-1] + [own[0]] + above[0]]
            )
            levels = levels.astype(jnp.int32).reshape(-1)
            plan = make_plan(me, meta, levels, line, blocks, count)
        for h in range(chunks):
            if tick == max(base, 3) if h == 0 else (h, line - 2) in hops.get(tick - 1, ()):
                gathered = below[h][::-1] + [own[h]] + above[h]
                for start in range(0, sizes[h], ROWS):
                    waiting.append((gathered, start, min(ROWS, sizes[h])))
        if flying and flying[0][0] < tick:
            _, mine, other = flying.pop(0)
            inflated = inflate(mine, other)
            opposite = send(tick, across, inflated)
            sources += [inflated, core(inflated), opposite, core(opposite)]
        if landed and landed[0][0] < tick:
            _, theirs, mine = landed.pop(0)
            flying.append((tick, mine, send(tick, pair, theirs)))
        many = len(waiting) if tick > max(hops) else 1
        for i, (gathered, start, rows) in enumerate(waiting[:many]):
            theirs, mine = product(me, plan, panel, gathered, line, start, rows)
            if i == 0:
                at(tick, theirs)
            landed.append((tick, theirs, mine))
        waiting = waiting[many:]
        tick += 1
    sizes = tuple(min(ROWS, size) for size in sizes for _ in range(0, size, ROWS))
    scale = float(4 * TR * width)
    owned = owned_tiles(me, meta, sources, sizes, count, scale)
    return owned[None, None]


def solution(mesh):
    placed = (
        P("row", "col", None, None, None),
        P("row", "col", None),
        P("row", "col", None),
        P("row", "col", None),
    )
    return jax.shard_map(
        functools.partial(on_device, mesh.shape["col"]),
        mesh=mesh,
        in_specs=placed,
        out_specs=P("row", "col", None, None, None),
        check_vma=False,
    )
```

```python
import functools

import jax
import jax.numpy as jnp
from jax import lax
from jax.experimental import pallas as pl
from jax.experimental.pallas import tpu as pltpu
from jax.sharding import PartitionSpec as P

TR = 8
CHUNKS = (128, 64, 64)
ROWS = (64, 64, 32)
FIELDS = 8
RING = 16
VMEM = 56 * 1024 * 1024


def arrival(q, source):
    steps = jnp.abs(source - q)
    link = (q + (source < q)) % 2
    return jnp.where(steps == 0, 0, 2 * steps - 1 + link)


def split(x):
    high = x.astype(jnp.bfloat16)
    low = (x - high.astype(jnp.float32)).astype(jnp.bfloat16)
    return high, low


def place_kernel(parts, *refs):
    o_ref, mark_ref = refs[-2:]
    mark_ref[...] = jnp.zeros_like(mark_ref)
    count = o_ref.shape[3]
    start = 0
    for x_ref in refs[:parts]:
        rows = x_ref.shape[0] // count
        for z in range(count):
            high, low = split(x_ref[z * rows : (z + 1) * rows])
            o_ref[0, 0, 0, z, 0, start : start + rows] = high
            o_ref[0, 0, 0, z, 1, start : start + rows] = low
        start += rows


def place(parts, buffer, group, relative, blocks, count):
    width = parts[0][0].shape[1]
    out = jax.ShapeDtypeStruct((2, blocks, 4, count, 2, width, width), jnp.bfloat16)
    in_specs = [
        pl.BlockSpec((count * rows, width), lambda j, first=first: (first // count + j, 0))
        for _, rows, first in parts
    ]
    args = [x for x, _, _ in parts]
    aliases = {}
    if buffer is not None:
        in_specs.append(pl.BlockSpec(memory_space=pl.ANY))
        args.append(buffer)
        aliases = {len(parts): 0}
    size = blocks * count * width * width
    return pl.pallas_call(
        functools.partial(place_kernel, len(parts)),
        grid=(blocks,),
        out_shape=(out, jax.ShapeDtypeStruct((8, 128), jnp.float32)),
        in_specs=in_specs,
        out_specs=(
            pl.BlockSpec(
                (1, 1, 1, count, 2, width, width), lambda j: (group, j, relative, 0, 0, 0, 0)
            ),
            pl.BlockSpec((8, 128), lambda j: (0, 0)),
        ),
        input_output_aliases=aliases,
        compiler_params=pltpu.CompilerParams(vmem_limit_bytes=VMEM),
        cost_estimate=pl.CostEstimate(flops=size, bytes_accessed=8 * size, transcendentals=0),
        name="place",
    )(*args)


def plan_kernel(line, blocks, count, me_ref, *refs):
    items = blocks * count
    known, shards = refs[:8], refs[8:-3]
    plan_ref, kept_ref, levels_ref = refs[-3:]
    r, c = me_ref[0], me_ref[1]
    q, p = c // 2, c % 2

    for i, shard in enumerate(shards):

        def note(j, _, i=i, shard=shard):
            levels_ref[i * items + j] = shard[0, j].astype(jnp.int32)
            return 0

        lax.fori_loop(0, items, note, 0)

    def write(n, tile, at, levels):
        plan_ref[FIELDS * n] = tile
        plan_ref[FIELDS * n + 1] = at
        for y in range(count):
            plan_ref[FIELDS * n + 2 + y] = levels(y)

    n = jnp.int32(0)
    for group in range(2):

        def column(j, n, group=group):
            row = group * blocks + j
            for relative in range(4):
                rr = jnp.bitwise_xor(r, relative)

                def entry(z, n, relative=relative, rr=rr):
                    noted = known[2 * relative + group][0, j * count + z]
                    k = rr * TR + noted.astype(jnp.int32)
                    ck = k // blocks
                    levels = arrival(q, ck // 2) * items + (k % blocks) * count
                    mine = ck % 2 == p
                    write(
                        n,
                        (row * 4 + relative) * count + z,
                        (ck // 2) * blocks + k % blocks,
                        lambda y: levels_ref[jnp.where(mine, levels + y, 0)],
                    )
                    return n + mine.astype(jnp.int32)

                n = lax.fori_loop(0, count, entry, n)
            write(n, row * 4 * count, line * blocks, lambda y: jnp.int32(0))
            n = n + n % 2
            kept_ref[FIELDS * row] = n
            for m in range(count):
                noted = known[group][0, items + j * count + m]
                kept_ref[FIELDS * row + 1 + m] = noted.astype(jnp.int32)
            return n

        n = lax.fori_loop(0, blocks, column, n)


def noted(x, row):
    return x, pl.BlockSpec((8, 128), lambda *_: (row // 8, 0), memory_space=pltpu.SMEM)


def make_plan(me, known, shards, line, blocks, count):
    smem = pl.BlockSpec(memory_space=pltpu.SMEM)
    args, specs = zip(*known, *shards)
    return pl.pallas_call(
        functools.partial(plan_kernel, line, blocks, count),
        grid=(1,),
        out_shape=(
            jax.ShapeDtypeStruct((FIELDS * (2 * blocks * 4 * count + 2),), jnp.int32),
            jax.ShapeDtypeStruct((FIELDS * 2 * blocks,), jnp.int32),
        ),
        in_specs=[smem, *specs],
        out_specs=(smem, smem),
        scratch_shapes=[pltpu.SMEM(((2 * line - 2) * blocks * count,), jnp.int32)],
        name="plan",
    )(me, *args)


def product_kernel(line, grid_blocks, part, me_ref, plan_ref, kept_ref, b_ref, *refs):
    parts = 2 * line - 2
    a_refs = refs[:parts]
    other_ref, own_ref, raw, halves, total, ring, a_sems, b_sems = refs[parts:]
    group, j = pl.program_id(0), pl.program_id(1)
    blocks, count, rows, width = (grid_blocks, *other_ref.shape[1:])
    size = blocks * count * rows
    last = 2 * blocks - 1
    row = group * blocks + j
    q = me_ref[1] // 2
    end = kept_ref[FIELDS * last]

    def fetch(n):
        tile = plan_ref[FIELDS * n]
        slot = n % RING
        return pltpu.make_async_copy(b_ref.at[tile], ring.at[slot], b_sems.at[slot])

    @pl.when(row == 0)
    def _():
        def each(act):
            for i in range(parts):
                steps, link = (i + 1) // 2, (i + 1) % 2
                source = q if i == 0 else jnp.where(q % 2 == link, q + steps, q - steps)

                @pl.when((source >= 0) & (source < line))
                def _():
                    rows_of = a_refs[i].at[part * size : (part + 1) * size]
                    to = raw.at[pl.ds(pl.multiple_of(source * size, size), size)]
                    act(pltpu.make_async_copy(rows_of, to, a_sems.at[i]))

        each(lambda copy: copy.start())

        def begin(n, _):
            fetch(n).start()
            return 0

        lax.fori_loop(0, jnp.minimum(end, RING), begin, 0)
        halves[line * blocks] = jnp.zeros(halves.shape[1:], halves.dtype)
        each(lambda copy: copy.wait())

        def convert(i, _):
            first = pl.multiple_of(i * count * rows, count * rows)
            high, low = split(raw[pl.ds(first, count * rows)])
            halves[i, 0 : count * rows] = high
            halves[i, count * rows :] = low
            return 0

        lax.fori_loop(0, line * blocks, convert, 0)

    total[...] = jnp.zeros_like(total)
    first = jnp.where(row == 0, 0, kept_ref[FIELDS * jnp.maximum(row - 1, 0)])

    def multiply(n):
        a = halves[plan_ref[FIELDS * n + 1]]
        slot = n % RING
        b_high, b_low = ring[slot, 0], ring[slot, 1]
        dot = functools.partial(jnp.dot, preferred_element_type=jnp.float32)
        by_high = dot(a, b_high)
        return by_high[: count * rows] + by_high[count * rows :] + dot(a[: count * rows], b_low)

    def step(i, _):
        n = first + 2 * i
        fetch(n).wait()
        fetch(n + 1).wait()
        products = [multiply(n), multiply(n + 1)]
        for e in range(2):
            for y in range(count):
                level = plan_ref[FIELDS * (n + e) + 2 + y]
                total[level] += products[e][y * rows : (y + 1) * rows]

        @pl.when(n + RING < end)
        def _():
            fetch(n + RING).start()
            fetch(n + RING + 1).start()

        return 0

    lax.fori_loop(0, (kept_ref[FIELDS * row] - first) // 2, step, 0)

    @pl.when(group == 0)
    def _():
        for m in range(count):
            other_ref[0, m] = total[kept_ref[FIELDS * row + 1 + m]]

    @pl.when(group == 1)
    def _():
        for m in range(count):
            own_ref[0, m] = total[kept_ref[FIELDS * row + 1 + m]]


def product(me, plan, panel, parts, line, part, rows):
    blocks, count, width = panel.shape[1], panel.shape[3], panel.shape[6]
    out = jax.ShapeDtypeStruct((blocks, count, rows, width), jnp.float32)
    smem = pl.BlockSpec(memory_space=pltpu.SMEM)
    return pl.pallas_call(
        functools.partial(product_kernel, line, blocks, part),
        grid=(2, blocks),
        out_shape=(out, out),
        in_specs=[smem] * 3 + [pl.BlockSpec(memory_space=pl.ANY)] * (1 + len(parts)),
        out_specs=(
            pl.BlockSpec(
                (1, count, rows, width), lambda g, j: (jnp.where(g == 0, j, blocks - 1), 0, 0, 0)
            ),
            pl.BlockSpec((1, count, rows, width), lambda g, j: (jnp.where(g == 0, 0, j), 0, 0, 0)),
        ),
        scratch_shapes=[
            pltpu.VMEM((line * blocks * count * rows, width), jnp.float32),
            pltpu.VMEM((line * blocks + 1, 2 * count * rows, width), jnp.bfloat16),
            pltpu.VMEM((TR, rows, width), jnp.float32),
            pltpu.VMEM((RING, 2, width, width), jnp.bfloat16),
            pltpu.SemaphoreType.DMA((len(parts),)),
            pltpu.SemaphoreType.DMA((RING,)),
        ],
        compiler_params=pltpu.CompilerParams(vmem_limit_bytes=VMEM),
        cost_estimate=pl.CostEstimate(
            flops=3 * 2 * 16 * blocks * count * rows * width * width,
            bytes_accessed=panel.size,
            transcendentals=0,
        ),
        name="product",
    )(me, *plan, panel.reshape(-1, 2, width, width), *parts)


def inflate_kernel(own_ref, other_ref, out_ref):
    count, rows = own_ref.shape[1:3]
    partial = jnp.zeros((8, own_ref.shape[3]), jnp.float32)
    for m in range(count):
        kept = own_ref[0, m] + other_ref[0, m]
        inflated = kept * kept
        out_ref[0, m * rows : (m + 1) * rows] = inflated
        for i in range(0, rows, 8):
            partial += inflated[i : i + 8]
    out_ref[0, count * rows :] = partial


def inflate(own, other):
    blocks, count, rows, width = own.shape
    spec = pl.BlockSpec((1, count, rows, width), lambda j: (j, 0, 0, 0))
    return pl.pallas_call(
        inflate_kernel,
        grid=(blocks,),
        out_shape=jax.ShapeDtypeStruct((blocks, count * rows + 8, width), jnp.float32),
        in_specs=[spec, spec],
        out_specs=pl.BlockSpec((1, count * rows + 8, width), lambda j: (j, 0, 0)),
        cost_estimate=pl.CostEstimate(
            flops=3 * own.size, bytes_accessed=12 * own.size, transcendentals=0
        ),
        name="inflate",
    )(own, other)


def owned_kernel(sizes, blocks, count, scale, me_ref, *refs):
    chunks = len(sizes)
    notes, refs = refs[:4], refs[4:]
    sources = refs[: 4 * chunks]
    out_ref, slots, partial, whose, in_sems, out_sems, sum_sems = refs[4 * chunks :]
    items = blocks * count
    most = items // 2
    r = me_ref[0]
    starts = [sum(sizes[:h]) for h in range(chunks)]

    def partials(act):
        for i in range(4 * chunks):
            rows = pl.ds(count * sizes[i // 4], 8)
            act(pltpu.make_async_copy(sources[i].at[:, rows], partial.at[i], sum_sems.at[i]))

    partials(lambda copy: copy.start())
    for s in range(4 * most):
        whose[s] = -1
    for relative in range(4):
        rr = jnp.bitwise_xor(r, relative)

        def place_item(f, n, relative=relative, rr=rr):
            mine = notes[relative][0, 2 * items + f].astype(jnp.int32) == r

            @pl.when(mine)
            def _():
                slot = rr * most + n
                whose[slot] = f // count
                for h in range(chunks):
                    pltpu.make_async_copy(
                        sources[4 * h + relative].at[
                            f // count, pl.ds(pl.multiple_of(f % count * sizes[h], 8), sizes[h])
                        ],
                        slots.at[slot, pl.ds(starts[h], sizes[h])],
                        in_sems.at[slot],
                    ).start()

            return n + mine.astype(jnp.int32)

        lax.fori_loop(0, items, place_item, jnp.int32(0))

    partials(lambda copy: copy.wait())
    factors = scale / jnp.sum(jnp.sum(partial[...], axis=0), axis=1)

    def finish(s, _):
        j = whose[s]

        @pl.when(j < 0)
        def _():
            slots[s] = jnp.zeros(slots.shape[1:], jnp.float32)

        for jj in range(blocks):

            @pl.when(j == jj)
            def _():
                pltpu.make_async_copy(slots.at[s], slots.at[s], in_sems.at[s]).wait()
                slots[s] = slots[s] * factors[jj : jj + 1]

        pltpu.make_async_copy(slots.at[s], out_ref.at[s], out_sems.at[s]).start()
        return 0

    lax.fori_loop(0, 4 * most, finish, 0)

    def drain(s, _):
        pltpu.make_async_copy(slots.at[s], out_ref.at[s], out_sems.at[s]).wait()
        return 0

    lax.fori_loop(0, 4 * most, drain, 0)


def owned_tiles(me, notes, sources, sizes, count, scale):
    blocks, _, width = sources[0].shape
    most = blocks * count // 2
    smem = pl.BlockSpec(memory_space=pltpu.SMEM)
    return pl.pallas_call(
        functools.partial(owned_kernel, sizes, blocks, count, scale),
        grid=(1,),
        out_shape=jax.ShapeDtypeStruct((4 * most, width, width), jnp.float32),
        in_specs=[smem, *(spec for _, spec in notes)]
        + [pl.BlockSpec(memory_space=pl.ANY)] * len(sources),
        out_specs=pl.BlockSpec(memory_space=pl.ANY),
        scratch_shapes=[
            pltpu.VMEM((4 * most, width, width), jnp.float32),
            pltpu.VMEM((len(sources), blocks, 8, width), jnp.float32),
            pltpu.SMEM((4 * most,), jnp.int32),
            pltpu.SemaphoreType.DMA((4 * most,)),
            pltpu.SemaphoreType.DMA((4 * most,)),
            pltpu.SemaphoreType.DMA((len(sources),)),
        ],
        compiler_params=pltpu.CompilerParams(vmem_limit_bytes=VMEM),
        cost_estimate=pl.CostEstimate(
            flops=4 * most * width * width,
            bytes_accessed=32 * most * width * width,
            transcendentals=0,
        ),
        name="owned",
    )(me, *(x for x, _ in notes), *sources)


def on_device(columns, matrix_tiles, tile_rows, keep_rows, owners):
    tiles = matrix_tiles[0]
    blocks, count, width = tiles.shape[0], tiles.shape[1], tiles.shape[2]
    line = columns // 2
    r, c = lax.axis_index("row"), lax.axis_index("col")
    me = jnp.stack([r, c]).astype(jnp.int32)

    core = functools.partial(lax.ppermute, axis_name="row", perm=[(i, i ^ 1) for i in range(4)])
    across = functools.partial(lax.ppermute, axis_name="row", perm=[(i, i ^ 2) for i in range(4)])
    pair = functools.partial(
        lax.ppermute, axis_name="col", perm=[(i, i ^ 1) for i in range(columns)]
    )

    links = []
    for first in (0, 1):
        perm = []
        for i in range(4 * columns):
            rank = i % columns // 2
            to = rank + 1 if rank % 2 == first else rank - 1
            inside = 0 <= to < line
            perm.append((i, i + 2 * (to - rank) if inside else i ^ columns))
        links.append(functools.partial(lax.ppermute, axis_name=("row", "col"), perm=perm))

    sizes = tuple(size * width // sum(CHUNKS) for size in CHUNKS)
    starts = [sum(sizes[:h]) for h in range(len(sizes))]

    chunks, half = len(sizes), width // 2
    rows = [size * width // sum(CHUNKS) for size in ROWS]

    def cut(x, h):
        x = x[:, :, starts[h] : starts[h] + sizes[h]]
        x = x.reshape(blocks * count, sizes[h] // rows[h], rows[h], width)
        return jnp.swapaxes(x, 0, 1).reshape(-1, width)

    notes = jnp.concatenate([tile_rows.reshape(-1), keep_rows.reshape(-1), owners.reshape(-1)])
    notes = jnp.pad(notes.astype(jnp.float32), (0, width - notes.shape[0]))
    own = [jnp.concatenate([cut(tiles, 0), jnp.broadcast_to(notes, (8, width))])]
    came = [[] for _ in sizes]

    ticks = {}

    def at(tick, x):
        ticks.setdefault(tick, []).append(x)
        return x

    def tie(x, *others):
        return lax.optimization_barrier((x, *others))[0] if others else x

    def after(tick, x):
        return tie(x, *ticks.get(tick - 1, ()))

    def send(tick, move, x, *more):
        return at(tick, move(after(tick, x), *more))

    swapped = []

    def swap(tick, x):
        x = tie(x, *swapped[-1:])
        swapped.append(send(tick, core, x))
        return swapped[-1]

    base = line - 1
    hops = {}
    for h in range(chunks):
        for hop in range(line - 1):
            if h == 0:
                tick = hop
            else:
                tick = base + hop + (h - 1 if hop else max(h - 2, 0))
            hops.setdefault(tick, []).append((h, hop))

    panel = None
    sources, waiting, landed, flying = [], [], [], []

    def put(tick, group, relative, *parts):
        nonlocal panel
        panel, mark = place(parts, panel, group, relative, blocks, count)
        at(tick, mark)

    items = blocks * count
    upper, parts = sizes[0] * items, sizes[0] // rows[0]

    def halves(top, low):
        return (*((top, rows[0], part * items) for part in range(parts)), (low, half, 0))

    tick = 0
    while tick <= max(hops) + 1 or landed or flying:
        for h, hop in hops.get(tick, ()):
            if hop:
                operands = came[h][-1], came[h][-2]
            else:
                operands = own[h], own[h]
            for link in range(1 if hop == line - 2 else 2):
                came[h].append(send(tick, links[link], operands[link]))
        if tick == 0:
            whole = tiles.reshape(-1, width)
            rest = tiles[:, :, half:].reshape(-1, width)
            b_pair, b_across = send(0, pair, own[0]), send(0, across, own[0])
            core_own = swap(0, whole)
            put(0, 1, 0, (whole, width, 0))
        if tick == 1:
            pair_rest, across_rest = send(1, pair, rest), send(1, across, rest)
            core_pair, core_notes = swap(1, b_pair), swap(1, own[0][upper:])
            put(1, 1, 1, (core_own, width, 0))
            later = after(1, tiles)
            own += [at(1, cut(later, h)) for h in range(1, chunks)]
        if tick == 2:
            diagonal, diagonal_rest = send(2, across, b_pair), send(2, pair, across_rest)
            core_across, core_pair_rest = swap(2, b_across), swap(2, pair_rest)
            core_across_rest = swap(2, across_rest)
            put(2, 0, 0, *halves(b_pair, pair_rest))
            put(2, 1, 2, *halves(b_across, across_rest))
            put(3, 0, 1, *halves(core_pair, core_pair_rest))
            put(3, 1, 3, *halves(core_across, core_across_rest))
        if tick == max(base, 3):
            core_diagonal = swap(tick, diagonal)
            put(tick, 0, 2, *halves(diagonal, diagonal_rest))
            put(tick, 0, 3, *halves(core_diagonal, swap(tick, diagonal_rest)))
            known = [
                (b_pair, upper),
                (own[0], upper),
                (core_pair, upper),
                (core_notes, 0),
                (diagonal, upper),
                (b_across, upper),
                (core_diagonal, upper),
                (core_across, upper),
            ]
            known = [noted(x, i) for x, i in known]
            shards = [noted(x, upper) for x in [own[0], *came[0]]]
            plan = make_plan(me, known, shards, line, blocks, count)
        for h in range(chunks):
            if tick == max(base, 3) if h == 0 else (h, line - 2) in hops.get(tick - 1, ()):
                gathered = [own[h], *came[h]]
                waiting += [(gathered, i, rows[h]) for i in range(sizes[h] // rows[h])]
        if flying and flying[0][0] < tick:
            _, mine, other = flying.pop(0)
            inflated = inflate(mine, other)
            opposite = send(tick, across, inflated)
            sources += [inflated, core(inflated), opposite, core(opposite)]
        if landed and landed[0][0] < tick:
            _, theirs, mine = landed.pop(0)
            other = send(tick, pair, theirs)
            flying.append((tick, mine, other))
        if waiting and tick < max(hops) - 1:
            gathered, part, size = waiting.pop(0)
            theirs, mine = product(me, plan, panel, gathered, line, part, size)
            landed.append((tick, at(tick, theirs), mine))
        tick += 1
    theirs, queue = None, []
    for n, (gathered, part, size) in enumerate(waiting):
        theirs, mine = product(
            me if theirs is None else tie(me, theirs), plan, panel, gathered, line, part, size
        )
        other = pair(tie(theirs, other))
        queue.append((mine, other))
        done = [theirs, *(waiting[n + 1][0] if n + 1 < len(waiting) else ())]
        if n == 0 and len(waiting) > 1:
            continue
        for mine, ready in queue if n + 1 == len(waiting) else [queue.pop(0)]:
            inflated = inflate(mine, tie(ready, *done) if ready is not other else ready)
            opposite = across(tie(inflated, opposite))
            sources += [inflated, core(inflated), opposite, core(opposite)]
    sizes = tuple(rows[h] for h in range(chunks) for _ in range(0, sizes[h], rows[h]))
    scale = float(4 * TR * width)
    owned = owned_tiles(me, known[1::2], sources, sizes, count, scale)
    return owned[None, None]


def solution(mesh):
    placed = (
        P("row", "col", None, None, None),
        P("row", "col", None),
        P("row", "col", None),
        P("row", "col", None),
    )
    return jax.shard_map(
        functools.partial(on_device, mesh.shape["col"]),
        mesh=mesh,
        in_specs=placed,
        out_specs=P("row", "col", None, None, None),
        check_vma=False,
    )
```

```python
import functools

import jax
import jax.numpy as jnp
from jax import lax
from jax.experimental import pallas as pl
from jax.experimental.pallas import tpu as pltpu
from jax.sharding import PartitionSpec as P

TR = 8
CHUNKS = (128, 64, 64)
ROWS = (64, 64, 32)
FIELDS = 8
RING = 16
VMEM = 56 * 1024 * 1024


def arrival(q, source):
    steps = jnp.abs(source - q)
    link = (q + (source < q)) % 2
    return jnp.where(steps == 0, 0, 2 * steps - 1 + link)


def split(x):
    high = x.astype(jnp.bfloat16)
    low = (x - high.astype(jnp.float32)).astype(jnp.bfloat16)
    return high, low


def place_kernel(parts, *refs):
    o_ref, mark_ref = refs[-2:]
    mark_ref[...] = jnp.zeros_like(mark_ref)
    count = o_ref.shape[3]
    start = 0
    for x_ref in refs[:parts]:
        rows = x_ref.shape[0] // count
        for z in range(count):
            high, low = split(x_ref[z * rows : (z + 1) * rows])
            o_ref[0, 0, 0, z, 0, start : start + rows] = high
            o_ref[0, 0, 0, z, 1, start : start + rows] = low
        start += rows


def place(parts, buffer, group, relative, blocks, count):
    width = parts[0][0].shape[1]
    out = jax.ShapeDtypeStruct((2, blocks, 4, count, 2, width, width), jnp.bfloat16)
    in_specs = [
        pl.BlockSpec((count * rows, width), lambda j, first=first: (first // count + j, 0))
        for _, rows, first in parts
    ]
    args = [x for x, _, _ in parts]
    aliases = {}
    if buffer is not None:
        in_specs.append(pl.BlockSpec(memory_space=pl.ANY))
        args.append(buffer)
        aliases = {len(parts): 0}
    size = blocks * count * width * width
    return pl.pallas_call(
        functools.partial(place_kernel, len(parts)),
        grid=(blocks,),
        out_shape=(out, jax.ShapeDtypeStruct((8, 128), jnp.float32)),
        in_specs=in_specs,
        out_specs=(
            pl.BlockSpec(
                (1, 1, 1, count, 2, width, width), lambda j: (group, j, relative, 0, 0, 0, 0)
            ),
            pl.BlockSpec((8, 128), lambda j: (0, 0)),
        ),
        input_output_aliases=aliases,
        compiler_params=pltpu.CompilerParams(vmem_limit_bytes=VMEM),
        cost_estimate=pl.CostEstimate(flops=size, bytes_accessed=8 * size, transcendentals=0),
        name="place",
    )(*args)


def plan_kernel(line, blocks, count, me_ref, *refs):
    items = blocks * count
    known, shards = refs[:8], refs[8:-3]
    plan_ref, kept_ref, levels_ref = refs[-3:]
    r, c = me_ref[0], me_ref[1]
    q, p = c // 2, c % 2

    for i, shard in enumerate(shards):

        def note(j, _, i=i, shard=shard):
            levels_ref[i * items + j] = shard[0, j].astype(jnp.int32)
            return 0

        lax.fori_loop(0, items, note, 0)

    def write(n, tile, at, levels):
        plan_ref[FIELDS * n] = tile
        plan_ref[FIELDS * n + 1] = at
        for y in range(count):
            plan_ref[FIELDS * n + 2 + y] = levels(y)

    n = jnp.int32(0)
    for group in range(2):

        def column(j, n, group=group):
            row = group * blocks + j
            for relative in range(4):
                rr = jnp.bitwise_xor(r, relative)

                def entry(z, n, relative=relative, rr=rr):
                    noted = known[2 * relative + group][0, j * count + z]
                    k = rr * TR + noted.astype(jnp.int32)
                    ck = k // blocks
                    levels = arrival(q, ck // 2) * items + (k % blocks) * count
                    mine = ck % 2 == p
                    write(
                        n,
                        (row * 4 + relative) * count + z,
                        (ck // 2) * blocks + k % blocks,
                        lambda y: levels_ref[jnp.where(mine, levels + y, 0)],
                    )
                    return n + mine.astype(jnp.int32)

                n = lax.fori_loop(0, count, entry, n)
            write(n, row * 4 * count, line * blocks, lambda y: jnp.int32(0))
            n = n + n % 2
            kept_ref[FIELDS * row] = n
            for m in range(count):
                noted = known[group][0, items + j * count + m]
                kept_ref[FIELDS * row + 1 + m] = noted.astype(jnp.int32)
            return n

        n = lax.fori_loop(0, blocks, column, n)


def noted(x, row):
    return x, pl.BlockSpec((8, 128), lambda *_: (row // 8, 0), memory_space=pltpu.SMEM)


def make_plan(me, known, shards, line, blocks, count):
    smem = pl.BlockSpec(memory_space=pltpu.SMEM)
    args, specs = zip(*known, *shards)
    return pl.pallas_call(
        functools.partial(plan_kernel, line, blocks, count),
        grid=(1,),
        out_shape=(
            jax.ShapeDtypeStruct((FIELDS * (2 * blocks * 4 * count + 2),), jnp.int32),
            jax.ShapeDtypeStruct((FIELDS * 2 * blocks,), jnp.int32),
        ),
        in_specs=[smem, *specs],
        out_specs=(smem, smem),
        scratch_shapes=[pltpu.SMEM(((2 * line - 2) * blocks * count,), jnp.int32)],
        name="plan",
    )(me, *args)


def product_kernel(line, groups, part, me_ref, plan_ref, kept_ref, b_ref, *refs):
    parts = 2 * line - 2
    a_refs = refs[:parts]
    out_refs, (raw, halves, total, ring, a_sems, b_sems) = refs[parts:-6], refs[-6:]
    blocks = (halves.shape[0] - 1) // line
    count, rows, width = out_refs[0].shape[1:]
    group, j = pl.program_id(0) + groups[0], pl.program_id(1)
    size = blocks * count * rows
    top, last = groups[0] * blocks, (groups[-1] + 1) * blocks - 1
    row = group * blocks + j
    q = me_ref[1] // 2
    begun = kept_ref[FIELDS * (top - 1)] if top else 0
    end = kept_ref[FIELDS * last]

    def fetch(n):
        tile = plan_ref[FIELDS * n]
        slot = n % RING
        return pltpu.make_async_copy(b_ref.at[tile], ring.at[slot], b_sems.at[slot])

    @pl.when(row == top)
    def _():
        def each(act):
            for i in range(parts):
                steps, link = (i + 1) // 2, (i + 1) % 2
                source = q if i == 0 else jnp.where(q % 2 == link, q + steps, q - steps)

                @pl.when((source >= 0) & (source < line))
                def _():
                    rows_of = a_refs[i].at[part * size : (part + 1) * size]
                    to = raw.at[pl.ds(pl.multiple_of(source * size, size), size)]
                    act(pltpu.make_async_copy(rows_of, to, a_sems.at[i]))

        each(lambda copy: copy.start())

        def begin(n, _):
            fetch(n).start()
            return 0

        lax.fori_loop(begun, jnp.minimum(end, begun + RING), begin, 0)
        halves[line * blocks] = jnp.zeros(halves.shape[1:], halves.dtype)
        each(lambda copy: copy.wait())

        def convert(i, _):
            first = pl.multiple_of(i * count * rows, count * rows)
            high, low = split(raw[pl.ds(first, count * rows)])
            halves[i, 0 : count * rows] = high
            halves[i, count * rows :] = low
            return 0

        lax.fori_loop(0, line * blocks, convert, 0)

    total[...] = jnp.zeros_like(total)
    first = jnp.where(row == top, begun, kept_ref[FIELDS * jnp.maximum(row - 1, 0)])

    def multiply(n):
        a = halves[plan_ref[FIELDS * n + 1]]
        slot = n % RING
        b_high, b_low = ring[slot, 0], ring[slot, 1]
        dot = functools.partial(jnp.dot, preferred_element_type=jnp.float32)
        by_high = dot(a, b_high)
        return by_high[: count * rows] + by_high[count * rows :] + dot(a[: count * rows], b_low)

    def step(i, _):
        n = first + 2 * i
        fetch(n).wait()
        fetch(n + 1).wait()
        products = [multiply(n), multiply(n + 1)]
        for e in range(2):
            for y in range(count):
                level = plan_ref[FIELDS * (n + e) + 2 + y]
                total[level] += products[e][y * rows : (y + 1) * rows]

        @pl.when(n + RING < end)
        def _():
            fetch(n + RING).start()
            fetch(n + RING + 1).start()

        return 0

    lax.fori_loop(0, (kept_ref[FIELDS * row] - first) // 2, step, 0)

    for g, out_ref in zip(groups, out_refs):

        @pl.when(group == g)
        def _():
            for m in range(count):
                out_ref[0, m] = total[kept_ref[FIELDS * row + 1 + m]]


def product(me, plan, panel, parts, line, part, rows, groups=(0, 1)):
    blocks, count, width = panel.shape[1], panel.shape[3], panel.shape[6]
    out = jax.ShapeDtypeStruct((blocks, count, rows, width), jnp.float32)
    smem = pl.BlockSpec(memory_space=pltpu.SMEM)
    return pl.pallas_call(
        functools.partial(product_kernel, line, groups, part),
        grid=(len(groups), blocks),
        out_shape=(out,) * len(groups),
        in_specs=[smem] * 3 + [pl.BlockSpec(memory_space=pl.ANY)] * (1 + len(parts)),
        out_specs=tuple(
            pl.BlockSpec(
                (1, count, rows, width),
                lambda g, j, i=i: (jnp.where(g == i, j, 0 if i else blocks - 1), 0, 0, 0),
            )
            for i in range(len(groups))
        ),
        scratch_shapes=[
            pltpu.VMEM((line * blocks * count * rows, width), jnp.float32),
            pltpu.VMEM((line * blocks + 1, 2 * count * rows, width), jnp.bfloat16),
            pltpu.VMEM((TR, rows, width), jnp.float32),
            pltpu.VMEM((RING, 2, width, width), jnp.bfloat16),
            pltpu.SemaphoreType.DMA((len(parts),)),
            pltpu.SemaphoreType.DMA((RING,)),
        ],
        compiler_params=pltpu.CompilerParams(vmem_limit_bytes=VMEM),
        cost_estimate=pl.CostEstimate(
            flops=3 * len(groups) * 16 * blocks * count * rows * width * width,
            bytes_accessed=len(groups) * panel.size // 2,
            transcendentals=0,
        ),
        name="product",
    )(me, *plan, panel.reshape(-1, 2, width, width), *parts)


def inflate_kernel(own_ref, other_ref, out_ref):
    blocks, count, rows, width = own_ref.shape
    for j in range(blocks):
        partial = jnp.zeros((8, width), jnp.float32)
        for m in range(count):
            kept = own_ref[j, m] + other_ref[j, m]
            inflated = kept * kept
            out_ref[j, m * rows : (m + 1) * rows] = inflated
            for i in range(0, rows, 8):
                partial += inflated[i : i + 8]
        out_ref[j, count * rows :] = partial


def inflate(own, other):
    blocks, count, rows, width = own.shape
    return pl.pallas_call(
        inflate_kernel,
        out_shape=jax.ShapeDtypeStruct((blocks, count * rows + 8, width), jnp.float32),
        compiler_params=pltpu.CompilerParams(vmem_limit_bytes=VMEM),
        cost_estimate=pl.CostEstimate(
            flops=3 * own.size, bytes_accessed=12 * own.size, transcendentals=0
        ),
        name="inflate",
    )(own, other)


def owned_kernel(sizes, blocks, count, scale, me_ref, *refs):
    chunks = len(sizes)
    notes, refs = refs[:4], refs[4:]
    sources = refs[: 4 * chunks]
    out_ref, slots, partial, whose, in_sems, out_sems, sum_sems = refs[4 * chunks :]
    items = blocks * count
    most = items // 2
    r = me_ref[0]
    starts = [sum(sizes[:h]) for h in range(chunks)]

    def partials(act):
        for i in range(4 * chunks):
            rows = pl.ds(count * sizes[i // 4], 8)
            act(pltpu.make_async_copy(sources[i].at[:, rows], partial.at[i], sum_sems.at[i]))

    partials(lambda copy: copy.start())
    for s in range(4 * most):
        whose[s] = -1
    for relative in range(4):
        rr = jnp.bitwise_xor(r, relative)

        def place_item(f, n, relative=relative, rr=rr):
            mine = notes[relative][0, 2 * items + f].astype(jnp.int32) == r

            @pl.when(mine)
            def _():
                slot = rr * most + n
                whose[slot] = f // count
                for h in range(chunks):
                    pltpu.make_async_copy(
                        sources[4 * h + relative].at[
                            f // count, pl.ds(pl.multiple_of(f % count * sizes[h], 8), sizes[h])
                        ],
                        slots.at[slot, pl.ds(starts[h], sizes[h])],
                        in_sems.at[slot],
                    ).start()

            return n + mine.astype(jnp.int32)

        lax.fori_loop(0, items, place_item, jnp.int32(0))

    partials(lambda copy: copy.wait())
    factors = scale / jnp.sum(jnp.sum(partial[...], axis=0), axis=1)

    def finish(s, _):
        j = whose[s]

        @pl.when(j < 0)
        def _():
            slots[s] = jnp.zeros(slots.shape[1:], jnp.float32)

        for jj in range(blocks):

            @pl.when(j == jj)
            def _():
                pltpu.make_async_copy(slots.at[s], slots.at[s], in_sems.at[s]).wait()
                slots[s] = slots[s] * factors[jj : jj + 1]

        pltpu.make_async_copy(slots.at[s], out_ref.at[s], out_sems.at[s]).start()
        return 0

    lax.fori_loop(0, 4 * most, finish, 0)

    def drain(s, _):
        pltpu.make_async_copy(slots.at[s], out_ref.at[s], out_sems.at[s]).wait()
        return 0

    lax.fori_loop(0, 4 * most, drain, 0)


def owned_tiles(me, notes, sources, sizes, count, scale):
    blocks, _, width = sources[0].shape
    most = blocks * count // 2
    smem = pl.BlockSpec(memory_space=pltpu.SMEM)
    return pl.pallas_call(
        functools.partial(owned_kernel, sizes, blocks, count, scale),
        grid=(1,),
        out_shape=jax.ShapeDtypeStruct((4 * most, width, width), jnp.float32),
        in_specs=[smem, *(spec for _, spec in notes)]
        + [pl.BlockSpec(memory_space=pl.ANY)] * len(sources),
        out_specs=pl.BlockSpec(memory_space=pl.ANY),
        scratch_shapes=[
            pltpu.VMEM((4 * most, width, width), jnp.float32),
            pltpu.VMEM((len(sources), blocks, 8, width), jnp.float32),
            pltpu.SMEM((4 * most,), jnp.int32),
            pltpu.SemaphoreType.DMA((4 * most,)),
            pltpu.SemaphoreType.DMA((4 * most,)),
            pltpu.SemaphoreType.DMA((len(sources),)),
        ],
        compiler_params=pltpu.CompilerParams(vmem_limit_bytes=VMEM),
        cost_estimate=pl.CostEstimate(
            flops=4 * most * width * width,
            bytes_accessed=32 * most * width * width,
            transcendentals=0,
        ),
        name="owned",
    )(me, *(x for x, _ in notes), *sources)


def on_device(columns, matrix_tiles, tile_rows, keep_rows, owners):
    tiles = matrix_tiles[0]
    blocks, count, width = tiles.shape[0], tiles.shape[1], tiles.shape[2]
    line = columns // 2
    r, c = lax.axis_index("row"), lax.axis_index("col")
    me = jnp.stack([r, c]).astype(jnp.int32)

    core = functools.partial(lax.ppermute, axis_name="row", perm=[(i, i ^ 1) for i in range(4)])
    across = functools.partial(lax.ppermute, axis_name="row", perm=[(i, i ^ 2) for i in range(4)])
    pair = functools.partial(
        lax.ppermute, axis_name="col", perm=[(i, i ^ 1) for i in range(columns)]
    )

    links = []
    for first in (0, 1):
        perm = []
        for i in range(4 * columns):
            rank = i % columns // 2
            to = rank + 1 if rank % 2 == first else rank - 1
            inside = 0 <= to < line
            perm.append((i, i + 2 * (to - rank) if inside else i ^ columns))
        links.append(functools.partial(lax.ppermute, axis_name=("row", "col"), perm=perm))

    sizes = tuple(size * width // sum(CHUNKS) for size in CHUNKS)
    starts = [sum(sizes[:h]) for h in range(len(sizes))]

    chunks, half = len(sizes), width // 2
    rows = [size * width // sum(CHUNKS) for size in ROWS]

    def cut(x, h):
        x = x[:, :, starts[h] : starts[h] + sizes[h]]
        x = x.reshape(blocks * count, sizes[h] // rows[h], rows[h], width)
        return jnp.swapaxes(x, 0, 1).reshape(-1, width)

    notes = jnp.concatenate([tile_rows.reshape(-1), keep_rows.reshape(-1), owners.reshape(-1)])
    notes = jnp.pad(notes.astype(jnp.float32), (0, width - notes.shape[0]))
    own = [jnp.concatenate([cut(tiles, 0), jnp.broadcast_to(notes, (8, width))])]
    came = [[] for _ in sizes]

    ticks = {}

    def at(tick, x):
        ticks.setdefault(tick, []).append(x)
        return x

    def tie(x, *others):
        return lax.optimization_barrier((x, *others))[0] if others else x

    def after(tick, x):
        return tie(x, *ticks.get(tick - 1, ()))

    def send(tick, move, x, *more):
        return at(tick, move(after(tick, x), *more))

    swapped = []

    def swap(tick, x):
        x = tie(x, *swapped[-1:])
        swapped.append(at(tick + 1, core(after(tick, x))))
        return swapped[-1]

    base = line - 1
    hops = {}
    for h in range(chunks):
        for hop in range(line - 1):
            if h == 0:
                tick = hop
            else:
                tick = base + hop + (h - 1 if hop else max(h - 2, 0))
            hops.setdefault(tick, []).append((h, hop))

    panel = None
    sources, waiting, landed, flying = [], [], [], []

    def put(tick, group, relative, *parts):
        nonlocal panel
        panel, mark = place(parts, panel, group, relative, blocks, count)
        at(tick, mark)

    items = blocks * count
    upper, parts = sizes[0] * items, sizes[0] // rows[0]

    def halves(top, low):
        return (*((top, rows[0], part * items) for part in range(parts)), (low, half, 0))

    tick = 0
    while tick <= max(hops) + 1 or landed or flying:
        if chunks > 1 and (1, line - 2) in hops.get(tick - 1, ()):
            gathered = [own[1], *came[1]]
            early, *_ = product(me, plan, panel, gathered, line, 0, rows[1], (0,))
            at(tick - 1, early)
        for h, hop in hops.get(tick, ()):
            if hop:
                operands = came[h][-1], came[h][-2]
            else:
                operands = own[h], own[h]
            for link in range(1 if hop == line - 2 else 2):
                came[h].append(send(tick, links[link], operands[link]))
        if tick == 0:
            whole = tiles.reshape(-1, width)
            rest = tie(tiles, own[0])[:, :, half:].reshape(-1, width)
            b_pair, b_across = send(0, pair, own[0]), send(0, across, own[0])
            core_own = swap(0, whole)
            put(0, 1, 0, (whole, width, 0))
        if tick == 1:
            pair_rest, across_rest = send(1, pair, rest), send(1, across, rest)
            core_pair, core_notes = swap(1, b_pair), swap(1, own[0][upper:])
            put(1, 1, 1, (core_own, width, 0))
            later = after(1, tiles)
            own += [at(1, cut(later, h)) for h in range(1, chunks)]
        if tick == 2:
            diagonal, diagonal_rest = send(2, across, b_pair), send(2, pair, across_rest)
            core_across, core_pair_rest = swap(2, b_across), swap(2, pair_rest)
            core_across_rest = swap(2, across_rest)
            put(2, 0, 0, *halves(b_pair, pair_rest))
            put(2, 1, 2, *halves(b_across, across_rest))
            put(3, 0, 1, *halves(core_pair, core_pair_rest))
            put(3, 1, 3, *halves(core_across, core_across_rest))
        if tick == max(base, 3):
            core_diagonal = swap(tick, diagonal)
            put(tick, 0, 2, *halves(diagonal, diagonal_rest))
            put(tick, 0, 3, *halves(core_diagonal, swap(tick, diagonal_rest)))
            known = [
                (b_pair, upper),
                (own[0], upper),
                (core_pair, upper),
                (core_notes, 0),
                (diagonal, upper),
                (b_across, upper),
                (core_diagonal, upper),
                (core_across, upper),
            ]
            known = [noted(x, i) for x, i in known]
            shards = [noted(x, upper) for x in [own[0], *came[0]]]
            plan = make_plan(me, known, shards, line, blocks, count)
        for h in range(chunks):
            if tick == max(base, 3) if h == 0 else (h, line - 2) in hops.get(tick - 1, ()):
                gathered = [own[h], *came[h]]
                waiting += [(gathered, i, rows[h]) for i in range(sizes[h] // rows[h])]
        if flying and flying[0][0] < tick:
            _, mine, other = flying.pop(0)
            inflated = inflate(mine, other)
            opposite = send(tick, across, inflated)
            sources += [inflated, core(inflated), opposite, core(opposite)]
        if landed and landed[0][0] < tick:
            _, theirs, mine = landed.pop(0)
            other = send(tick, pair, theirs)
            flying.append((tick, mine, other))
        if waiting and tick < max(hops) - 1:
            gathered, part, size = waiting.pop(0)
            theirs, mine = product(me, plan, panel, gathered, line, part, size)
            landed.append((tick, at(tick, theirs), mine))
        tick += 1
    theirs, last = [early], early
    for gathered, part, size in waiting[1:]:
        last, *_ = product(tie(me, last), plan, panel, gathered, line, part, size, (0,))
        theirs.append(last)
    last = early
    for n, (gathered, part, size) in enumerate(waiting):
        last = theirs[-1] if n == 1 else last
        last, *_ = product(tie(me, last), plan, panel, gathered, line, part, size, (1,))
        other = pair(tie(theirs[n], other))
        inflated = inflate(last, other)
        opposite = across(tie(inflated, opposite))
        sources += [inflated, core(inflated), opposite, core(opposite)]
    sizes = tuple(rows[h] for h in range(chunks) for _ in range(0, sizes[h], rows[h]))
    scale = float(4 * TR * width)
    owned = owned_tiles(me, known[1::2], sources, sizes, count, scale)
    return owned[None, None]


def solution(mesh):
    placed = (
        P("row", "col", None, None, None),
        P("row", "col", None),
        P("row", "col", None),
        P("row", "col", None),
    )
    return jax.shard_map(
        functools.partial(on_device, mesh.shape["col"]),
        mesh=mesh,
        in_specs=placed,
        out_specs=P("row", "col", None, None, None),
        check_vma=False,
    )
```

```python
import functools

import jax
import jax.numpy as jnp
from jax import lax
from jax.experimental import pallas as pl
from jax.experimental.pallas import tpu as pltpu
from jax.sharding import PartitionSpec as P

TR = 8
CHUNKS = (128, 64, 64)
ROWS = (64, 64, 64)
PIECES = 2
FIELDS = 8
ALL, EARLY, FINAL = 0, 1, 2
RING = 16
VMEM = 56 * 1024 * 1024


def arrival(q, source):
    steps = jnp.abs(source - q)
    link = (q + (source < q)) % 2
    return jnp.where(steps == 0, 0, 2 * steps - 1 + link)


def split(x):
    high = x.astype(jnp.bfloat16)
    low = (x - high.astype(jnp.float32)).astype(jnp.bfloat16)
    return high, low


def place_kernel(parts, *refs):
    o_ref, mark_ref = refs[-2:]
    mark_ref[...] = jnp.zeros_like(mark_ref)
    count = o_ref.shape[3]
    start = 0
    for x_ref in refs[:parts]:
        rows = x_ref.shape[0] // count
        for z in range(count):
            high, low = split(x_ref[z * rows : (z + 1) * rows])
            o_ref[0, 0, 0, z, 0, start : start + rows] = high
            o_ref[0, 0, 0, z, 1, start : start + rows] = low
        start += rows


def place(parts, buffer, group, relative, blocks, count):
    width = parts[0][0].shape[1]
    out = jax.ShapeDtypeStruct((2, blocks, 4, count, 2, width, width), jnp.bfloat16)
    in_specs = [
        pl.BlockSpec((count * rows, width), lambda j, first=first: (first // count + j, 0))
        for _, rows, first in parts
    ]
    args = [x for x, _, _ in parts]
    aliases = {}
    if buffer is not None:
        in_specs.append(pl.BlockSpec(memory_space=pl.ANY))
        args.append(buffer)
        aliases = {len(parts): 0}
    size = blocks * count * width * width
    return pl.pallas_call(
        functools.partial(place_kernel, len(parts)),
        grid=(blocks,),
        out_shape=(out, jax.ShapeDtypeStruct((8, 128), jnp.float32)),
        in_specs=in_specs,
        out_specs=(
            pl.BlockSpec(
                (1, 1, 1, count, 2, width, width), lambda j: (group, j, relative, 0, 0, 0, 0)
            ),
            pl.BlockSpec((8, 128), lambda j: (0, 0)),
        ),
        input_output_aliases=aliases,
        compiler_params=pltpu.CompilerParams(vmem_limit_bytes=VMEM),
        cost_estimate=pl.CostEstimate(flops=size, bytes_accessed=8 * size, transcendentals=0),
        name="place",
    )(*args)


def plan_kernel(line, blocks, count, me_ref, *refs):
    items = blocks * count
    room = listed(blocks, count)
    known, shards = refs[:8], refs[8:-3]
    plan_ref, kept_ref, levels_ref = refs[-3:]
    r, c = me_ref[0], me_ref[1]
    q, p = c // 2, c % 2

    for i, shard in enumerate(shards):

        def note(j, _, i=i, shard=shard):
            levels = jnp.int32(0)
            for y in range(count):
                levels += shard[0, j * count + y].astype(jnp.int32) << (4 * y)
            levels_ref[i * blocks + j] = levels
            return 0

        lax.fori_loop(0, blocks, note, 0)

    def write(n, tile, at, levels):
        plan_ref[FIELDS * n] = tile
        plan_ref[FIELDS * n + 1] = at
        plan_ref[FIELDS * n + 2] = levels

    ends = tuple(jnp.int32(i * room) for i in range(3))
    for group in range(2):

        def column(j, ends, group=group):
            row = group * blocks + j
            for relative in range(4):
                rr = jnp.bitwise_xor(r, relative)

                def entry(z, ends, relative=relative, rr=rr):
                    noted = known[2 * relative + group][0, j * count + z]
                    k = rr * TR + noted.astype(jnp.int32)
                    ck = k // blocks
                    mine = ck % 2 == p
                    came = jnp.where(mine, arrival(q, ck // 2), 0)
                    final = came == 2 * line - 3
                    tile = (row * 4 + relative) * count + z
                    at = (ck // 2) * blocks + k % blocks
                    levels = levels_ref[came * blocks + k % blocks]
                    write(ends[0], tile, at, levels)
                    write(jnp.where(final, ends[2], ends[1]), tile, at, levels)
                    return (
                        ends[0] + mine.astype(jnp.int32),
                        ends[1] + (mine & ~final).astype(jnp.int32),
                        ends[2] + (mine & final).astype(jnp.int32),
                    )

                ends = lax.fori_loop(0, count, entry, ends)
            filled = []
            for i, n in enumerate(ends):
                write(n, row * 4 * count, line * blocks, jnp.int32(0))
                filled.append(n + n % 2)
                kept_ref[FIELDS * (i * 2 * blocks + row)] = filled[-1]
            for m in range(count):
                noted = known[group][0, items + j * count + m]
                kept_ref[FIELDS * row + 1 + m] = noted.astype(jnp.int32)
            return tuple(filled)

        ends = lax.fori_loop(0, blocks, column, ends)


def listed(blocks, count):
    return 2 * blocks * (4 * count + 1) + 2


def noted(x, row):
    return x, pl.BlockSpec((8, 128), lambda *_: (row // 8, 0), memory_space=pltpu.SMEM)


def make_plan(me, known, shards, line, blocks, count):
    smem = pl.BlockSpec(memory_space=pltpu.SMEM)
    args, specs = zip(*known, *shards)
    return pl.pallas_call(
        functools.partial(plan_kernel, line, blocks, count),
        grid=(1,),
        out_shape=(
            jax.ShapeDtypeStruct((3 * FIELDS * listed(blocks, count),), jnp.int32),
            jax.ShapeDtypeStruct((3 * FIELDS * 2 * blocks,), jnp.int32),
        ),
        in_specs=[smem, *specs],
        out_specs=(smem, smem),
        scratch_shapes=[pltpu.SMEM(((2 * line - 2) * blocks,), jnp.int32)],
        name="plan",
    )(me, *args)


def product_kernel(line, which, arrivals, pieces, part, me_ref, plan_ref, kept_ref, b_ref, *refs):
    a_refs, refs = refs[: len(arrivals)], refs[len(arrivals) :]
    before, refs = (refs[:2], refs[2:]) if which == FINAL else ((), refs)
    out_refs, (raw, halves, total, ring, a_sems, b_sems) = refs[:-6], refs[-6:]
    blocks = (halves.shape[0] - 1) // line
    count, piece, width = out_refs[0].shape[1:]
    rows = pieces * piece
    group, j = pl.program_id(0), pl.program_id(1)
    size = blocks * count * rows
    row = group * blocks + j
    q = me_ref[1] // 2
    begun = which * listed(blocks, count)
    ends = which * 2 * blocks
    end = kept_ref[FIELDS * (ends + 2 * blocks - 1)]

    def fetch(n):
        tile = plan_ref[FIELDS * n]
        slot = n % RING
        return pltpu.make_async_copy(b_ref.at[tile], ring.at[slot], b_sems.at[slot])

    @pl.when(row == 0)
    def _():
        def each(act):
            for n, i in enumerate(arrivals):
                steps, link = (i + 1) // 2, (i + 1) % 2
                source = q if i == 0 else jnp.where(q % 2 == link, q + steps, q - steps)

                @pl.when((source >= 0) & (source < line))
                def _():
                    rows_of = a_refs[n].at[part * size : (part + 1) * size]
                    to = raw.at[pl.ds(pl.multiple_of(source * size, size), size)]
                    act(pltpu.make_async_copy(rows_of, to, a_sems.at[n]), source)

        each(lambda copy, _: copy.start())

        def begin(n, _):
            fetch(n).start()
            return 0

        lax.fori_loop(begun, jnp.minimum(end, begun + RING), begin, 0)
        halves[line * blocks] = jnp.zeros(halves.shape[1:], halves.dtype)

        def convert(i, _):
            first = pl.multiple_of(i * count * rows, count * rows)
            high, low = split(raw[pl.ds(first, count * rows)])
            halves[i, 0 : count * rows] = high
            halves[i, count * rows :] = low
            return 0

        def use(copy, source):
            copy.wait()
            lax.fori_loop(source * blocks, (source + 1) * blocks, convert, 0)

        each(use)

    total[...] = jnp.zeros_like(total)
    first = jnp.where(row == 0, begun, kept_ref[FIELDS * (ends + jnp.maximum(row - 1, 0))])

    def multiply(n):
        a = halves[plan_ref[FIELDS * n + 1]]
        slot = n % RING
        b_high, b_low = ring[slot, 0], ring[slot, 1]
        dot = functools.partial(jnp.dot, preferred_element_type=jnp.float32)
        by_high = dot(a, b_high)
        return by_high[: count * rows] + by_high[count * rows :] + dot(a[: count * rows], b_low)

    def step(i, _):
        n = first + 2 * i
        fetch(n).wait()
        fetch(n + 1).wait()
        products = [multiply(n), multiply(n + 1)]
        for e in range(2):
            levels = plan_ref[FIELDS * (n + e) + 2]
            for y in range(count):
                level = (levels >> (4 * y)) & 15
                total[level] += products[e][y * rows : (y + 1) * rows]

        @pl.when(n + RING < end)
        def _():
            fetch(n + RING).start()
            fetch(n + RING + 1).start()

        return 0

    lax.fori_loop(0, (kept_ref[FIELDS * (ends + row)] - first) // 2, step, 0)

    for g in range(2):

        @pl.when(group == g)
        def _():
            for m in range(count):
                level = kept_ref[FIELDS * row + 1 + m]
                for n in range(pieces):
                    some = pl.ds(n * piece, piece)
                    result = total[level, some]
                    if before:
                        result += before[g][0, m, some]
                    out_refs[g * pieces + n][0, m] = result


def product(me, plan, panel, parts, line, part, rows, which=ALL, before=(), pieces=1):
    blocks, count, width = panel.shape[1], panel.shape[3], panel.shape[6]
    arrivals = list(range(2 * line - 2))
    arrivals = {ALL: arrivals, EARLY: arrivals[:-1], FINAL: arrivals[-1:]}[which]
    out = jax.ShapeDtypeStruct((blocks, count, rows // pieces, width), jnp.float32)
    smem = pl.BlockSpec(memory_space=pltpu.SMEM)

    def tiles_of(group, size):
        return pl.BlockSpec(
            (1, count, size, width),
            lambda g, j: (jnp.where(g == group, j, 0 if group else blocks - 1), 0, 0, 0),
        )

    return pl.pallas_call(
        functools.partial(product_kernel, line, which, arrivals, pieces, part),
        grid=(2, blocks),
        out_shape=(out,) * (2 * pieces),
        in_specs=[smem] * 3
        + [pl.BlockSpec(memory_space=pl.ANY)] * (1 + len(arrivals))
        + [tiles_of(g, rows) for g in range(len(before))],
        out_specs=tuple(tiles_of(g, rows // pieces) for g in range(2) for _ in range(pieces)),
        scratch_shapes=[
            pltpu.VMEM((line * blocks * count * rows, width), jnp.float32),
            pltpu.VMEM((line * blocks + 1, 2 * count * rows, width), jnp.bfloat16),
            pltpu.VMEM((TR, rows, width), jnp.float32),
            pltpu.VMEM((RING, 2, width, width), jnp.bfloat16),
            pltpu.SemaphoreType.DMA((len(arrivals),)),
            pltpu.SemaphoreType.DMA((RING,)),
        ],
        compiler_params=pltpu.CompilerParams(vmem_limit_bytes=VMEM),
        cost_estimate=pl.CostEstimate(
            flops=3 * 32 * blocks * count * rows * width * width * len(arrivals) // (2 * line - 2),
            bytes_accessed=panel.size * len(arrivals) // (2 * line - 2),
            transcendentals=0,
        ),
        name="product",
    )(me, *plan, panel.reshape(-1, 2, width, width), *(parts[i] for i in arrivals), *before)


def inflate_kernel(own_ref, other_ref, out_ref):
    blocks, count, rows, width = own_ref.shape
    for j in range(blocks):
        partial = jnp.zeros((8, width), jnp.float32)
        for m in range(count):
            kept = own_ref[j, m] + other_ref[j, m]
            inflated = kept * kept
            out_ref[j, m * rows : (m + 1) * rows] = inflated
            for i in range(0, rows, 8):
                partial += inflated[i : i + 8]
        out_ref[j, count * rows :] = partial


def inflate(own, other):
    blocks, count, rows, width = own.shape
    return pl.pallas_call(
        inflate_kernel,
        out_shape=jax.ShapeDtypeStruct((blocks, count * rows + 8, width), jnp.float32),
        compiler_params=pltpu.CompilerParams(vmem_limit_bytes=VMEM),
        cost_estimate=pl.CostEstimate(
            flops=3 * own.size, bytes_accessed=12 * own.size, transcendentals=0
        ),
        name="inflate",
    )(own, other)


def owned_kernel(sizes, blocks, count, scale, me_ref, *refs):
    chunks = len(sizes)
    notes, refs = refs[:4], refs[4:]
    sources = refs[: 4 * chunks]
    out_ref, slots, partial, whose, in_sems, out_sems, sum_sems = refs[4 * chunks :]
    items = blocks * count
    most = items // 2
    r = me_ref[0]
    starts = [sum(sizes[:h]) for h in range(chunks)]

    def partials(act):
        for i in range(4 * chunks):
            rows = pl.ds(count * sizes[i // 4], 8)
            act(pltpu.make_async_copy(sources[i].at[:, rows], partial.at[i], sum_sems.at[i]))

    partials(lambda copy: copy.start())
    for s in range(4 * most):
        whose[s] = -1
    for relative in range(4):
        rr = jnp.bitwise_xor(r, relative)

        def place_item(f, n, relative=relative, rr=rr):
            mine = notes[relative][0, 2 * items + f].astype(jnp.int32) == r

            @pl.when(mine)
            def _():
                slot = rr * most + n
                whose[slot] = f // count
                for h in range(chunks):
                    pltpu.make_async_copy(
                        sources[4 * h + relative].at[
                            f // count, pl.ds(pl.multiple_of(f % count * sizes[h], 8), sizes[h])
                        ],
                        slots.at[slot, pl.ds(starts[h], sizes[h])],
                        in_sems.at[slot],
                    ).start()

            return n + mine.astype(jnp.int32)

        lax.fori_loop(0, items, place_item, jnp.int32(0))

    partials(lambda copy: copy.wait())
    factors = scale / jnp.sum(jnp.sum(partial[...], axis=0), axis=1)

    def finish(s, _):
        j = whose[s]

        @pl.when(j < 0)
        def _():
            slots[s] = jnp.zeros(slots.shape[1:], jnp.float32)

        for jj in range(blocks):

            @pl.when(j == jj)
            def _():
                pltpu.make_async_copy(slots.at[s], slots.at[s], in_sems.at[s]).wait()
                slots[s] = slots[s] * factors[jj : jj + 1]

        pltpu.make_async_copy(slots.at[s], out_ref.at[s], out_sems.at[s]).start()
        return 0

    lax.fori_loop(0, 4 * most, finish, 0)

    def drain(s, _):
        pltpu.make_async_copy(slots.at[s], out_ref.at[s], out_sems.at[s]).wait()
        return 0

    lax.fori_loop(0, 4 * most, drain, 0)


def owned_tiles(me, notes, sources, sizes, count, scale):
    blocks, _, width = sources[0].shape
    most = blocks * count // 2
    smem = pl.BlockSpec(memory_space=pltpu.SMEM)
    return pl.pallas_call(
        functools.partial(owned_kernel, sizes, blocks, count, scale),
        grid=(1,),
        out_shape=jax.ShapeDtypeStruct((4 * most, width, width), jnp.float32),
        in_specs=[smem, *(spec for _, spec in notes)]
        + [pl.BlockSpec(memory_space=pl.ANY)] * len(sources),
        out_specs=pl.BlockSpec(memory_space=pl.ANY),
        scratch_shapes=[
            pltpu.VMEM((4 * most, width, width), jnp.float32),
            pltpu.VMEM((len(sources), blocks, 8, width), jnp.float32),
            pltpu.SMEM((4 * most,), jnp.int32),
            pltpu.SemaphoreType.DMA((4 * most,)),
            pltpu.SemaphoreType.DMA((4 * most,)),
            pltpu.SemaphoreType.DMA((len(sources),)),
        ],
        compiler_params=pltpu.CompilerParams(vmem_limit_bytes=VMEM),
        cost_estimate=pl.CostEstimate(
            flops=4 * most * width * width,
            bytes_accessed=32 * most * width * width,
            transcendentals=0,
        ),
        name="owned",
    )(me, *(x for x, _ in notes), *sources)


def on_device(columns, matrix_tiles, tile_rows, keep_rows, owners):
    tiles = matrix_tiles[0]
    blocks, count, width = tiles.shape[0], tiles.shape[1], tiles.shape[2]
    line = columns // 2
    r, c = lax.axis_index("row"), lax.axis_index("col")
    me = jnp.stack([r, c]).astype(jnp.int32)

    core = functools.partial(lax.ppermute, axis_name="row", perm=[(i, i ^ 1) for i in range(4)])
    across = functools.partial(lax.ppermute, axis_name="row", perm=[(i, i ^ 2) for i in range(4)])
    pair = functools.partial(
        lax.ppermute, axis_name="col", perm=[(i, i ^ 1) for i in range(columns)]
    )

    links = []
    for first in (0, 1):
        perm = []
        for i in range(4 * columns):
            rank = i % columns // 2
            to = rank + 1 if rank % 2 == first else rank - 1
            inside = 0 <= to < line
            perm.append((i, i + 2 * (to - rank) if inside else i ^ columns))
        links.append(functools.partial(lax.ppermute, axis_name=("row", "col"), perm=perm))

    sizes = tuple(size * width // sum(CHUNKS) for size in CHUNKS)
    starts = [sum(sizes[:h]) for h in range(len(sizes))]

    chunks, half = len(sizes), width // 2
    rows = [size * width // sum(CHUNKS) for size in ROWS]

    def cut(x, h):
        x = x[:, :, starts[h] : starts[h] + sizes[h]]
        x = x.reshape(blocks * count, sizes[h] // rows[h], rows[h], width)
        return jnp.swapaxes(x, 0, 1).reshape(-1, width)

    notes = jnp.concatenate([tile_rows.reshape(-1), keep_rows.reshape(-1), owners.reshape(-1)])
    notes = jnp.pad(notes.astype(jnp.float32), (0, width - notes.shape[0]))
    own = [jnp.concatenate([cut(tiles, 0), jnp.broadcast_to(notes, (8, width))])]
    came = [[] for _ in sizes]

    ticks = {}

    def at(tick, x):
        ticks.setdefault(tick, []).append(x)
        return x

    def tie(x, *others):
        return lax.optimization_barrier((x, *others))[0] if others else x

    def after(tick, x):
        return tie(x, *ticks.get(tick - 1, ()))

    def send(tick, move, x, *more):
        return at(tick, move(after(tick, x), *more))

    def swap(tick, x, *others):
        return at(tick + 1, core(after(tick, tie(x, *others))))

    base = line - 1
    hops = {}
    for h in range(chunks):
        for hop in range(line - 1):
            if h == 0:
                tick = hop
            else:
                tick = base + hop + (h - 1 if hop else max(h - 2, 0))
            hops.setdefault(tick, []).append((h, hop))

    panel = None
    sources, waiting, landed, flying = [], [], [], []
    begun, made, cuts = {}, [], [1] * (chunks - 1) + [PIECES]

    def put(tick, group, relative, *parts):
        nonlocal panel
        panel, mark = place(parts, panel, group, relative, blocks, count)
        at(tick, mark)

    items = blocks * count
    upper, parts = sizes[0] * items, sizes[0] // rows[0]

    def halves(top, low):
        return (*((top, rows[0], part * items) for part in range(parts)), (low, half, 0))

    tick = 0
    while tick <= max(hops) + 1 or landed or flying:
        for h in range(1, chunks):
            if (h, line - 2) in hops.get(tick - 1, ()):
                results = product(
                    me, plan, panel, [own[h], *came[h]], line, 0, rows[h], FINAL, begun[h], cuts[h]
                )
                at(tick - 1, results[0])
                made.append((results[: cuts[h]], results[cuts[h] :]))
        for h, hop in hops.get(tick, ()):
            if hop:
                operands = came[h][-1], came[h][-2]
            else:
                operands = own[h], own[h]
            for link in range(1 if hop == line - 2 else 2):
                came[h].append(send(tick, links[link], operands[link]))
            if h and hop == line - 2:
                begun[h] = product(
                    me, plan, panel, [own[h], *came[h][:-1]], line, 0, rows[h], EARLY
                )
                at(tick, begun[h][0])
        if tick == 0:
            whole = tiles.reshape(-1, width)
            rest = tie(tiles, own[0])[:, :, half:].reshape(-1, width)
            b_pair, b_across = send(0, pair, own[0]), send(0, across, own[0])
            core_own = swap(0, whole)
            put(0, 1, 0, *halves(own[0], rest))
        if tick == 1:
            pair_rest, across_rest = send(1, pair, rest), send(1, across, rest)
            core_pair = swap(1, b_pair)
            put(1, 1, 1, (core_own, width, 0))
            later = after(1, tiles)
            own += [at(1, cut(later, h)) for h in range(1, chunks)]
        if tick == 2:
            diagonal, diagonal_rest = send(2, across, b_pair), send(2, pair, across_rest)
            core_across, core_pair_rest = swap(2, b_across), swap(2, pair_rest)
            core_across_rest = swap(2, across_rest, core_across)
            core_notes = swap(2, own[0][upper:], core_pair_rest)
            put(2, 0, 0, *halves(b_pair, pair_rest))
            put(2, 1, 2, *halves(b_across, across_rest))
            put(3, 0, 1, *halves(core_pair, core_pair_rest))
            put(3, 1, 3, *halves(core_across, core_across_rest))
        if tick == max(base, 3):
            core_diagonal = swap(tick, diagonal)
            put(tick, 0, 2, *halves(diagonal, diagonal_rest))
            core_diagonal_rest = swap(tick, diagonal_rest, core_diagonal)
            put(tick, 0, 3, *halves(core_diagonal, core_diagonal_rest))
            known = [
                (b_pair, upper),
                (own[0], upper),
                (core_pair, upper),
                (core_notes, 0),
                (diagonal, upper),
                (b_across, upper),
                (core_diagonal, upper),
                (core_across, upper),
            ]
            known = [noted(x, i) for x, i in known]
            shards = [noted(x, upper) for x in [own[0], *came[0]]]
            plan = make_plan(me, known, shards, line, blocks, count)
            gathered = [own[0], *came[0]]
            waiting = [(gathered, i, rows[0]) for i in range(parts)]
        if flying and flying[0][0] < tick:
            _, mine, other = flying.pop(0)
            inflated = inflate(mine, other)
            opposite = send(tick, across, inflated)
            sources += [inflated, core(inflated), opposite, core(opposite)]
        if landed and landed[0][0] < tick:
            _, theirs, mine = landed.pop(0)
            other = send(tick, pair, theirs)
            flying.append((tick, mine, other))
        if waiting:
            gathered, part, size = waiting.pop(0)
            theirs, mine = product(me, plan, panel, gathered, line, part, size)
            landed.append((tick, at(tick, theirs), mine))
        tick += 1
    for theirs, mine in made:
        for x, y in zip(theirs, mine):
            other = pair(tie(x, other))
            inflated = inflate(y, other)
            opposite = across(tie(inflated, opposite))
            sources += [inflated, core(inflated), opposite, core(opposite)]
    sizes = tuple(
        rows[h] // cuts[h]
        for h in range(chunks)
        for _ in range(0, sizes[h], rows[h] // cuts[h])
    )
    scale = float(4 * TR * width)
    owned = owned_tiles(me, known[1::2], sources, sizes, count, scale)
    return owned[None, None]


def solution(mesh):
    placed = (
        P("row", "col", None, None, None),
        P("row", "col", None),
        P("row", "col", None),
        P("row", "col", None),
    )
    return jax.shard_map(
        functools.partial(on_device, mesh.shape["col"]),
        mesh=mesh,
        in_specs=placed,
        out_specs=P("row", "col", None, None, None),
        check_vma=False,
    )
```

```python
import functools

import jax
import jax.numpy as jnp
from jax import lax
from jax.experimental import pallas as pl
from jax.experimental.pallas import tpu as pltpu
from jax.sharding import PartitionSpec as P

TR = 8
CHUNKS = (128, 64, 64)
ROWS = (64, 64, 64)
CUTS = (1, 1, 1)
FIELDS = 8
ALL, EARLY, FINAL = 0, 1, 2
RING = 16
COLUMNS = 2
VMEM = 56 * 1024 * 1024


def arrival(q, source):
    steps = jnp.abs(source - q)
    link = (q + (source < q)) % 2
    return jnp.where(steps == 0, 0, 2 * steps - 1 + link)


def split(x):
    high = x.astype(jnp.bfloat16)
    low = (x - high.astype(jnp.float32)).astype(jnp.bfloat16)
    return high, low


def place_kernel(parts, *refs):
    o_ref, mark_ref = refs[-2:]
    mark_ref[...] = jnp.zeros_like(mark_ref)
    count = o_ref.shape[3]
    start = 0
    for x_ref in refs[:parts]:
        rows = x_ref.shape[0] // count
        for z in range(count):
            high, low = split(x_ref[z * rows : (z + 1) * rows])
            o_ref[0, 0, 0, z, 0, start : start + rows] = high
            o_ref[0, 0, 0, z, 1, start : start + rows] = low
        start += rows


def place(parts, buffer, group, relative, blocks, count):
    width = parts[0][0].shape[1]
    out = jax.ShapeDtypeStruct((2, blocks, 4, count, 2, width, width), jnp.bfloat16)
    in_specs = [
        pl.BlockSpec((count * rows, width), lambda j, first=first: (first // count + j, 0))
        for _, rows, first in parts
    ]
    args = [x for x, _, _ in parts]
    aliases = {}
    if buffer is not None:
        in_specs.append(pl.BlockSpec(memory_space=pl.ANY))
        args.append(buffer)
        aliases = {len(parts): 0}
    size = blocks * count * width * width
    return pl.pallas_call(
        functools.partial(place_kernel, len(parts)),
        grid=(blocks,),
        out_shape=(out, jax.ShapeDtypeStruct((8, 128), jnp.float32)),
        in_specs=in_specs,
        out_specs=(
            pl.BlockSpec(
                (1, 1, 1, count, 2, width, width), lambda j: (group, j, relative, 0, 0, 0, 0)
            ),
            pl.BlockSpec((8, 128), lambda j: (0, 0)),
        ),
        input_output_aliases=aliases,
        compiler_params=pltpu.CompilerParams(vmem_limit_bytes=VMEM),
        cost_estimate=pl.CostEstimate(flops=size, bytes_accessed=8 * size, transcendentals=0),
        name="place",
    )(*args)


def plan_kernel(line, blocks, count, me_ref, *refs):
    items = blocks * count
    room = listed(blocks, count)
    known, shards = refs[:8], refs[8:-3]
    plan_ref, kept_ref, levels_ref = refs[-3:]
    r, c = me_ref[0], me_ref[1]
    q, p = c // 2, c % 2

    for i, shard in enumerate(shards):

        def note(j, _, i=i, shard=shard):
            levels = jnp.int32(0)
            for y in range(count):
                levels += shard[0, j * count + y].astype(jnp.int32) << (4 * y)
            levels_ref[i * blocks + j] = levels
            return 0

        lax.fori_loop(0, blocks, note, 0)

    def write(n, tile, at, levels):
        plan_ref[FIELDS * n] = tile
        plan_ref[FIELDS * n + 1] = at
        plan_ref[FIELDS * n + 2] = levels

    ends = tuple(jnp.int32(i * room) for i in range(3))
    for group in range(2):

        def column(j, ends, group=group):
            row = group * blocks + j
            for relative in range(4):
                rr = jnp.bitwise_xor(r, relative)

                def entry(z, ends, relative=relative, rr=rr):
                    noted = known[2 * relative + group][0, j * count + z]
                    k = rr * TR + noted.astype(jnp.int32)
                    ck = k // blocks
                    mine = ck % 2 == p
                    came = jnp.where(mine, arrival(q, ck // 2), 0)
                    final = came == 2 * line - 3
                    tile = (row * 4 + relative) * count + z
                    at = (ck // 2) * blocks + k % blocks
                    levels = levels_ref[came * blocks + k % blocks]
                    write(ends[0], tile, at, levels)
                    write(jnp.where(final, ends[2], ends[1]), tile, at, levels)
                    return (
                        ends[0] + mine.astype(jnp.int32),
                        ends[1] + (mine & ~final).astype(jnp.int32),
                        ends[2] + (mine & final).astype(jnp.int32),
                    )

                ends = lax.fori_loop(0, count, entry, ends)
            filled = []
            for i, n in enumerate(ends):
                write(n, row * 4 * count, line * blocks, jnp.int32(0))
                filled.append(n + n % 2)
                kept_ref[FIELDS * (i * 2 * blocks + row)] = filled[-1]
            for m in range(count):
                noted = known[group][0, items + j * count + m]
                kept_ref[FIELDS * row + 1 + m] = noted.astype(jnp.int32)
            return tuple(filled)

        ends = lax.fori_loop(0, blocks, column, ends)


def listed(blocks, count):
    return 2 * blocks * (4 * count + 1) + 2


def noted(x, row):
    return x, pl.BlockSpec((8, 128), lambda *_: (row // 8, 0), memory_space=pltpu.SMEM)


def make_plan(me, known, shards, line, blocks, count):
    smem = pl.BlockSpec(memory_space=pltpu.SMEM)
    args, specs = zip(*known, *shards)
    return pl.pallas_call(
        functools.partial(plan_kernel, line, blocks, count),
        grid=(1,),
        out_shape=(
            jax.ShapeDtypeStruct((3 * FIELDS * listed(blocks, count),), jnp.int32),
            jax.ShapeDtypeStruct((3 * FIELDS * 2 * blocks,), jnp.int32),
        ),
        in_specs=[smem, *specs],
        out_specs=(smem, smem),
        scratch_shapes=[pltpu.SMEM(((2 * line - 2) * blocks,), jnp.int32)],
        name="plan",
    )(me, *args)


def product_kernel(line, which, arrivals, pieces, part, me_ref, plan_ref, kept_ref, b_ref, *refs):
    a_refs, refs = refs[: len(arrivals)], refs[len(arrivals) :]
    before, refs = (refs[:2], refs[2:]) if which == FINAL else ((), refs)
    out_refs, (raw, halves, total, ring, a_sems, b_sems) = refs[:-6], refs[-6:]
    blocks = (halves.shape[0] - 1) // line
    count, piece, width = out_refs[0].shape[1:]
    rows = pieces * piece
    group, j = pl.program_id(0), pl.program_id(1)
    size = blocks * count * rows
    columns = out_refs[0].shape[0]
    q = me_ref[1] // 2
    begun = which * listed(blocks, count)
    ends = which * 2 * blocks
    end = kept_ref[FIELDS * (ends + 2 * blocks - 1)]

    def fetch(n):
        tile = plan_ref[FIELDS * n]
        slot = n % RING
        return pltpu.make_async_copy(b_ref.at[tile], ring.at[slot], b_sems.at[slot])

    @pl.when((group == 0) & (j == 0))
    def _():
        def each(act):
            for n, i in enumerate(arrivals):
                steps, link = (i + 1) // 2, (i + 1) % 2
                source = q if i == 0 else jnp.where(q % 2 == link, q + steps, q - steps)

                @pl.when((source >= 0) & (source < line))
                def _():
                    rows_of = a_refs[n].at[part * size : (part + 1) * size]
                    to = raw.at[pl.ds(pl.multiple_of(source * size, size), size)]
                    act(pltpu.make_async_copy(rows_of, to, a_sems.at[n]), source)

        each(lambda copy, _: copy.start())

        def begin(n, _):
            fetch(n).start()
            return 0

        lax.fori_loop(begun, jnp.minimum(end, begun + RING), begin, 0)
        halves[line * blocks] = jnp.zeros(halves.shape[1:], halves.dtype)

        def convert(i, _):
            first = pl.multiple_of(i * count * rows, count * rows)
            high, low = split(raw[pl.ds(first, count * rows)])
            halves[i, 0 : count * rows] = high
            halves[i, count * rows :] = low
            return 0

        def use(copy, source):
            copy.wait()
            lax.fori_loop(source * blocks, (source + 1) * blocks, convert, 0)

        each(use)

    def multiply(n):
        a = halves[plan_ref[FIELDS * n + 1]]
        slot = n % RING
        b_high, b_low = ring[slot, 0], ring[slot, 1]
        dot = functools.partial(jnp.dot, preferred_element_type=jnp.float32)
        by_high = dot(a, b_high)
        return by_high[: count * rows] + by_high[count * rows :] + dot(a[: count * rows], b_low)

    def step(first, i):
        n = first + 2 * i
        fetch(n).wait()
        fetch(n + 1).wait()
        products = [multiply(n), multiply(n + 1)]
        for e in range(2):
            levels = plan_ref[FIELDS * (n + e) + 2]
            for y in range(count):
                level = (levels >> (4 * y)) & 15
                total[level] += products[e][y * rows : (y + 1) * rows]

        @pl.when(n + RING < end)
        def _():
            fetch(n + RING).start()
            fetch(n + RING + 1).start()

        return first

    for u in range(columns):
        row = group * blocks + j * columns + u
        first = jnp.where(row == 0, begun, kept_ref[FIELDS * (ends + jnp.maximum(row - 1, 0))])
        total[...] = jnp.zeros_like(total)
        lax.fori_loop(
            0,
            (kept_ref[FIELDS * (ends + row)] - first) // 2,
            lambda i, first: step(first, i),
            first,
        )
        for g in range(2):

            @pl.when(group == g)
            def _():
                for m in range(count):
                    level = kept_ref[FIELDS * row + 1 + m]
                    for n in range(pieces):
                        some = pl.ds(n * piece, piece)
                        result = total[level, some]
                        if before:
                            result += before[g][u, m, some]
                        out_refs[g * pieces + n][u, m] = result


def product(me, plan, panel, parts, line, part, rows, which=ALL, before=(), pieces=1):
    blocks, count, width = panel.shape[1], panel.shape[3], panel.shape[6]
    arrivals = list(range(2 * line - 2))
    arrivals = {ALL: arrivals, EARLY: arrivals[:-1], FINAL: arrivals[-1:]}[which]
    out = jax.ShapeDtypeStruct((blocks, count, rows // pieces, width), jnp.float32)
    smem = pl.BlockSpec(memory_space=pltpu.SMEM)

    columns = min(COLUMNS, blocks)
    steps = blocks // columns

    def tiles_of(group, size):
        return pl.BlockSpec(
            (columns, count, size, width),
            lambda g, j: (jnp.where(g == group, j, 0 if group else steps - 1), 0, 0, 0),
        )

    return pl.pallas_call(
        functools.partial(product_kernel, line, which, arrivals, pieces, part),
        grid=(2, steps),
        out_shape=(out,) * (2 * pieces),
        in_specs=[smem] * 3
        + [pl.BlockSpec(memory_space=pl.ANY)] * (1 + len(arrivals))
        + [tiles_of(g, rows) for g in range(len(before))],
        out_specs=tuple(tiles_of(g, rows // pieces) for g in range(2) for _ in range(pieces)),
        scratch_shapes=[
            pltpu.VMEM((line * blocks * count * rows, width), jnp.float32),
            pltpu.VMEM((line * blocks + 1, 2 * count * rows, width), jnp.bfloat16),
            pltpu.VMEM((TR, rows, width), jnp.float32),
            pltpu.VMEM((RING, 2, width, width), jnp.bfloat16),
            pltpu.SemaphoreType.DMA((len(arrivals),)),
            pltpu.SemaphoreType.DMA((RING,)),
        ],
        compiler_params=pltpu.CompilerParams(vmem_limit_bytes=VMEM),
        cost_estimate=pl.CostEstimate(
            flops=3 * 32 * blocks * count * rows * width * width * len(arrivals) // (2 * line - 2),
            bytes_accessed=panel.size * len(arrivals) // (2 * line - 2),
            transcendentals=0,
        ),
        name="product",
    )(me, *plan, panel.reshape(-1, 2, width, width), *(parts[i] for i in arrivals), *before)


def inflate_kernel(own_ref, other_ref, out_ref):
    blocks, count, rows, width = own_ref.shape
    for j in range(blocks):
        partial = jnp.zeros((8, width), jnp.float32)
        for m in range(count):
            kept = own_ref[j, m] + other_ref[j, m]
            inflated = kept * kept
            out_ref[j, m * rows : (m + 1) * rows] = inflated
            for i in range(0, rows, 8):
                partial += inflated[i : i + 8]
        out_ref[j, count * rows :] = partial


def inflate(own, other):
    blocks, count, rows, width = own.shape
    return pl.pallas_call(
        inflate_kernel,
        out_shape=jax.ShapeDtypeStruct((blocks, count * rows + 8, width), jnp.float32),
        compiler_params=pltpu.CompilerParams(vmem_limit_bytes=VMEM),
        cost_estimate=pl.CostEstimate(
            flops=3 * own.size, bytes_accessed=12 * own.size, transcendentals=0
        ),
        name="inflate",
    )(own, other)


def owned_kernel(sizes, blocks, count, scale, me_ref, *refs):
    chunks = len(sizes)
    notes, refs = refs[:4], refs[4:]
    sources = refs[: 4 * chunks]
    out_ref, slots, partial, whose, in_sems, out_sems, sum_sems = refs[4 * chunks :]
    items = blocks * count
    most = items // 2
    r = me_ref[0]
    starts = [sum(sizes[:h]) for h in range(chunks)]

    def partials(act):
        for i in range(4 * chunks):
            rows = pl.ds(count * sizes[i // 4], 8)
            act(pltpu.make_async_copy(sources[i].at[:, rows], partial.at[i], sum_sems.at[i]))

    partials(lambda copy: copy.start())
    for s in range(4 * most):
        whose[s] = -1
    for relative in range(4):
        rr = jnp.bitwise_xor(r, relative)

        def place_item(f, n, relative=relative, rr=rr):
            mine = notes[relative][0, 2 * items + f].astype(jnp.int32) == r

            @pl.when(mine)
            def _():
                slot = rr * most + n
                whose[slot] = f // count
                for h in range(chunks):
                    pltpu.make_async_copy(
                        sources[4 * h + relative].at[
                            f // count, pl.ds(pl.multiple_of(f % count * sizes[h], 8), sizes[h])
                        ],
                        slots.at[slot, pl.ds(starts[h], sizes[h])],
                        in_sems.at[slot],
                    ).start()

            return n + mine.astype(jnp.int32)

        lax.fori_loop(0, items, place_item, jnp.int32(0))

    partials(lambda copy: copy.wait())
    factors = scale / jnp.sum(jnp.sum(partial[...], axis=0), axis=1)

    def finish(s, _):
        j = whose[s]

        @pl.when(j < 0)
        def _():
            slots[s] = jnp.zeros(slots.shape[1:], jnp.float32)

        for jj in range(blocks):

            @pl.when(j == jj)
            def _():
                pltpu.make_async_copy(slots.at[s], slots.at[s], in_sems.at[s]).wait()
                slots[s] = slots[s] * factors[jj : jj + 1]

        pltpu.make_async_copy(slots.at[s], out_ref.at[s], out_sems.at[s]).start()
        return 0

    lax.fori_loop(0, 4 * most, finish, 0)

    def drain(s, _):
        pltpu.make_async_copy(slots.at[s], out_ref.at[s], out_sems.at[s]).wait()
        return 0

    lax.fori_loop(0, 4 * most, drain, 0)


def owned_tiles(me, notes, sources, sizes, count, scale):
    blocks, _, width = sources[0].shape
    most = blocks * count // 2
    smem = pl.BlockSpec(memory_space=pltpu.SMEM)
    return pl.pallas_call(
        functools.partial(owned_kernel, sizes, blocks, count, scale),
        grid=(1,),
        out_shape=jax.ShapeDtypeStruct((4 * most, width, width), jnp.float32),
        in_specs=[smem, *(spec for _, spec in notes)]
        + [pl.BlockSpec(memory_space=pl.ANY)] * len(sources),
        out_specs=pl.BlockSpec(memory_space=pl.ANY),
        scratch_shapes=[
            pltpu.VMEM((4 * most, width, width), jnp.float32),
            pltpu.VMEM((len(sources), blocks, 8, width), jnp.float32),
            pltpu.SMEM((4 * most,), jnp.int32),
            pltpu.SemaphoreType.DMA((4 * most,)),
            pltpu.SemaphoreType.DMA((4 * most,)),
            pltpu.SemaphoreType.DMA((len(sources),)),
        ],
        compiler_params=pltpu.CompilerParams(vmem_limit_bytes=VMEM),
        cost_estimate=pl.CostEstimate(
            flops=4 * most * width * width,
            bytes_accessed=32 * most * width * width,
            transcendentals=0,
        ),
        name="owned",
    )(me, *(x for x, _ in notes), *sources)


def on_device(columns, matrix_tiles, tile_rows, keep_rows, owners):
    tiles = matrix_tiles[0]
    blocks, count, width = tiles.shape[0], tiles.shape[1], tiles.shape[2]
    line = columns // 2
    r, c = lax.axis_index("row"), lax.axis_index("col")
    me = jnp.stack([r, c]).astype(jnp.int32)

    core = functools.partial(lax.ppermute, axis_name="row", perm=[(i, i ^ 1) for i in range(4)])
    across = functools.partial(lax.ppermute, axis_name="row", perm=[(i, i ^ 2) for i in range(4)])
    pair = functools.partial(
        lax.ppermute, axis_name="col", perm=[(i, i ^ 1) for i in range(columns)]
    )

    links = []
    for first in (0, 1):
        perm = []
        for i in range(4 * columns):
            rank = i % columns // 2
            to = rank + 1 if rank % 2 == first else rank - 1
            inside = 0 <= to < line
            perm.append((i, i + 2 * (to - rank) if inside else i ^ columns))
        links.append(functools.partial(lax.ppermute, axis_name=("row", "col"), perm=perm))

    sizes = tuple(size * width // sum(CHUNKS) for size in CHUNKS)
    starts = [sum(sizes[:h]) for h in range(len(sizes))]

    chunks, half = len(sizes), width // 2
    rows = [size * width // sum(CHUNKS) for size in ROWS]

    def cut(x, h):
        x = x[:, :, starts[h] : starts[h] + sizes[h]]
        x = x.reshape(blocks * count, sizes[h] // rows[h], rows[h], width)
        return jnp.swapaxes(x, 0, 1).reshape(-1, width)

    notes = jnp.concatenate([tile_rows.reshape(-1), keep_rows.reshape(-1), owners.reshape(-1)])
    notes = jnp.pad(notes.astype(jnp.float32), (0, width - notes.shape[0]))
    own = [jnp.concatenate([cut(tiles, 0), jnp.broadcast_to(notes, (8, width))])]
    came = [[] for _ in sizes]

    ticks = {}

    def at(tick, x):
        ticks.setdefault(tick, []).append(x)
        return x

    def tie(x, *others):
        return lax.optimization_barrier((x, *others))[0] if others else x

    def after(tick, x):
        return tie(x, *ticks.get(tick - 1, ()))

    def send(tick, move, x, *more):
        return at(tick, move(after(tick, x), *more))

    def swap(tick, x, *others):
        return at(tick + 1, core(after(tick, tie(x, *others))))

    base = line - 1
    hops = {}
    for h in range(chunks):
        for hop in range(line - 1):
            if h == 0:
                tick = hop
            else:
                tick = base + hop + (h - 1 if hop else max(h - 2, 0))
            hops.setdefault(tick, []).append((h, hop))

    panel = None
    sources, waiting, landed, flying = [], [], [], []
    begun, made, cuts = {}, [], CUTS

    def put(tick, group, relative, *parts):
        nonlocal panel
        panel, mark = place(parts, panel, group, relative, blocks, count)
        at(tick, mark)

    items = blocks * count
    upper, parts = sizes[0] * items, sizes[0] // rows[0]

    def halves(top, low, number=0):
        upper_rows = ((top, rows[0], part * items) for part in range(parts))
        return (*upper_rows, (low, half, number * items))

    tick = 0
    while tick <= max(hops) + 1 or landed or flying:
        for h in range(1, chunks):
            if (h, line - 2) in hops.get(tick - 1, ()):
                results = product(
                    me, plan, panel, [own[h], *came[h]], line, 0, rows[h], FINAL, begun[h], cuts[h]
                )
                at(tick - 1, results[0])
                made.append((results[: cuts[h]], results[cuts[h] :]))
        for h, hop in hops.get(tick, ()):
            if hop:
                operands = came[h][-1], came[h][-2]
            else:
                operands = own[h], own[h]
            for link in range(1 if hop == line - 2 else 2):
                came[h].append(send(tick, links[link], operands[link]))
            if h and hop == line - 2:
                begun[h] = product(
                    me, plan, panel, [own[h], *came[h][:-1]], line, 0, rows[h], EARLY
                )
                at(tick, begun[h][0])
        if tick == 0:
            whole = tiles.reshape(-1, width)
            rest = tie(tiles, own[0])[:, :, half:].reshape(-1, width)
            b_pair, b_across = send(0, pair, own[0]), send(0, across, own[0])
            core_own = swap(0, whole)
            put(0, 1, 0, *halves(own[0], rest))
        if tick == 1:
            pair_rest, across_rest = send(1, pair, rest), send(1, across, rest)
            core_pair = at(1, swap(1, b_pair))
            put(1, 1, 1, (core_own, width, 0))
            later = after(1, tiles)
            own += [at(1, cut(later, h)) for h in range(1, chunks)]
        if tick == 2:
            diagonal, diagonal_rest = send(2, across, b_pair), send(2, pair, across_rest)
            core_across = swap(2, b_across)
            core_rest = swap(2, jnp.concatenate([pair_rest, across_rest, own[0][upper:]]))
            put(2, 0, 0, *halves(b_pair, pair_rest))
            put(2, 1, 2, *halves(b_across, across_rest))
            put(2, 0, 1, *halves(core_pair, core_rest))
            put(2, 1, 3, *halves(core_across, core_rest, 1))
        if tick == max(base, 3):
            core_diagonal = swap(tick, diagonal)
            put(tick, 0, 2, *halves(diagonal, diagonal_rest))
            core_diagonal_rest = swap(tick, diagonal_rest, core_diagonal)
            put(tick, 0, 3, *halves(core_diagonal, core_diagonal_rest))
            known = [
                (b_pair, upper),
                (own[0], upper),
                (core_pair, upper),
                (core_rest, 2 * half * items),
                (diagonal, upper),
                (b_across, upper),
                (core_diagonal, upper),
                (core_across, upper),
            ]
            known = [noted(x, i) for x, i in known]
            shards = [noted(x, upper) for x in [own[0], *came[0]]]
            plan = make_plan(me, known, shards, line, blocks, count)
            gathered = [own[0], *came[0]]
            waiting = [(gathered, i, rows[0]) for i in range(parts)]
        if flying and flying[0][0] < tick:
            _, mine, other = flying.pop(0)
            inflated = inflate(mine, other)
            opposite = send(tick, across, inflated)
            sources += [inflated, core(inflated), opposite, core(opposite)]
        if landed and landed[0][0] < tick:
            _, theirs, mine = landed.pop(0)
            other = send(tick, pair, theirs)
            flying.append((tick, mine, other))
        if waiting:
            gathered, part, size = waiting.pop(0)
            theirs, mine = product(me, plan, panel, gathered, line, part, size)
            landed.append((tick, at(tick, theirs), mine))
        tick += 1
    for theirs, mine in made:
        others = [pair(tie(x, other)) for x in theirs]
        other = others[-1]
        inflated = []
        for x, y in zip(mine, others):
            inflated.append(inflate(x, tie(y, *inflated[-1:])))
        for x in inflated:
            opposite = across(tie(x, opposite))
            sources += [x, core(x), opposite, core(opposite)]
    sizes = tuple(
        rows[h] // cuts[h]
        for h in range(chunks)
        for _ in range(0, sizes[h], rows[h] // cuts[h])
    )
    scale = float(4 * TR * width)
    owned = owned_tiles(me, known[1::2], sources, sizes, count, scale)
    return owned[None, None]


def solution(mesh):
    placed = (
        P("row", "col", None, None, None),
        P("row", "col", None),
        P("row", "col", None),
        P("row", "col", None),
    )
    return jax.shard_map(
        functools.partial(on_device, mesh.shape["col"]),
        mesh=mesh,
        in_specs=placed,
        out_specs=P("row", "col", None, None, None),
        check_vma=False,
    )
```

```python
import functools

import jax
import jax.numpy as jnp
from jax import lax
from jax.experimental import pallas as pl
from jax.experimental.pallas import tpu as pltpu
from jax.sharding import PartitionSpec as P

TR = 8
CHUNKS = (128, 64, 64)
ROWS = (64, 64, 64)
CUTS = (1, 1, 1)
FIELDS = 8
ALL, EARLY, FINAL = 0, 1, 2
RING = 16
COLUMNS = 2
VMEM = 56 * 1024 * 1024


def arrival(q, source):
    steps = jnp.abs(source - q)
    link = (q + (source < q)) % 2
    return jnp.where(steps == 0, 0, 2 * steps - 1 + link)


def split(x):
    high = x.astype(jnp.bfloat16)
    low = (x - high.astype(jnp.float32)).astype(jnp.bfloat16)
    return high, low


def place_kernel(parts, *refs):
    o_ref, mark_ref = refs[-2:]
    mark_ref[...] = jnp.zeros_like(mark_ref)
    count = o_ref.shape[3]
    start = 0
    for x_ref in refs[:parts]:
        rows = x_ref.shape[0] // count
        for z in range(count):
            high, low = split(x_ref[z * rows : (z + 1) * rows])
            o_ref[0, 0, 0, z, 0, start : start + rows] = high
            o_ref[0, 0, 0, z, 1, start : start + rows] = low
        start += rows


def place(parts, buffer, group, relative, blocks, count):
    width = parts[0][0].shape[1]
    out = jax.ShapeDtypeStruct((2, blocks, 4, count, 2, width, width), jnp.bfloat16)
    in_specs = [
        pl.BlockSpec((count * rows, width), lambda j, first=first: (first // count + j, 0))
        for _, rows, first in parts
    ]
    args = [x for x, _, _ in parts]
    aliases = {}
    if buffer is not None:
        in_specs.append(pl.BlockSpec(memory_space=pl.ANY))
        args.append(buffer)
        aliases = {len(parts): 0}
    size = blocks * count * width * width
    return pl.pallas_call(
        functools.partial(place_kernel, len(parts)),
        grid=(blocks,),
        out_shape=(out, jax.ShapeDtypeStruct((8, 128), jnp.float32)),
        in_specs=in_specs,
        out_specs=(
            pl.BlockSpec(
                (1, 1, 1, count, 2, width, width), lambda j: (group, j, relative, 0, 0, 0, 0)
            ),
            pl.BlockSpec((8, 128), lambda j: (0, 0)),
        ),
        input_output_aliases=aliases,
        compiler_params=pltpu.CompilerParams(vmem_limit_bytes=VMEM),
        cost_estimate=pl.CostEstimate(flops=size, bytes_accessed=8 * size, transcendentals=0),
        name="place",
    )(*args)


def plan_kernel(line, blocks, count, me_ref, *refs):
    items = blocks * count
    room = listed(blocks, count)
    known, shards = refs[:8], refs[8:-3]
    plan_ref, kept_ref, levels_ref = refs[-3:]
    r, c = me_ref[0], me_ref[1]
    q, p = c // 2, c % 2

    for i, shard in enumerate(shards):

        def note(j, _, i=i, shard=shard):
            levels = jnp.int32(0)
            for y in range(count):
                levels += shard[0, j * count + y].astype(jnp.int32) << (4 * y)
            levels_ref[i * blocks + j] = levels
            return 0

        lax.fori_loop(0, blocks, note, 0)

    def write(n, tile, at, levels):
        plan_ref[FIELDS * n] = tile
        plan_ref[FIELDS * n + 1] = at
        plan_ref[FIELDS * n + 2] = levels

    ends = tuple(jnp.int32(i * room) for i in range(3))
    for group in range(2):

        def column(j, ends, group=group):
            row = group * blocks + j
            for relative in range(4):
                rr = jnp.bitwise_xor(r, relative)

                def entry(z, ends, relative=relative, rr=rr):
                    noted = known[2 * relative + group][0, j * count + z]
                    k = rr * TR + noted.astype(jnp.int32)
                    ck = k // blocks
                    mine = ck % 2 == p
                    came = jnp.where(mine, arrival(q, ck // 2), 0)
                    final = came == 2 * line - 3
                    tile = (row * 4 + relative) * count + z
                    at = (ck // 2) * blocks + k % blocks
                    levels = levels_ref[came * blocks + k % blocks]
                    write(ends[0], tile, at, levels)
                    write(jnp.where(final, ends[2], ends[1]), tile, at, levels)
                    return (
                        ends[0] + mine.astype(jnp.int32),
                        ends[1] + (mine & ~final).astype(jnp.int32),
                        ends[2] + (mine & final).astype(jnp.int32),
                    )

                ends = lax.fori_loop(0, count, entry, ends)
            filled = []
            for i, n in enumerate(ends):
                write(n, row * 4 * count, line * blocks, jnp.int32(0))
                filled.append(n + n % 2)
                kept_ref[FIELDS * (i * 2 * blocks + row)] = filled[-1]
            for m in range(count):
                noted = known[group][0, items + j * count + m]
                kept_ref[FIELDS * row + 1 + m] = noted.astype(jnp.int32)
            return tuple(filled)

        ends = lax.fori_loop(0, blocks, column, ends)


def listed(blocks, count):
    return 2 * blocks * (4 * count + 1) + 2


def noted(x, row):
    return x, pl.BlockSpec((8, 128), lambda *_: (row // 8, 0), memory_space=pltpu.SMEM)


def make_plan(me, known, shards, line, blocks, count):
    smem = pl.BlockSpec(memory_space=pltpu.SMEM)
    args, specs = zip(*known, *shards)
    return pl.pallas_call(
        functools.partial(plan_kernel, line, blocks, count),
        grid=(1,),
        out_shape=(
            jax.ShapeDtypeStruct((3 * FIELDS * listed(blocks, count),), jnp.int32),
            jax.ShapeDtypeStruct((3 * FIELDS * 2 * blocks,), jnp.int32),
        ),
        in_specs=[smem, *specs],
        out_specs=(smem, smem),
        scratch_shapes=[pltpu.SMEM(((2 * line - 2) * blocks,), jnp.int32)],
        name="plan",
    )(me, *args)


def product_kernel(line, which, arrivals, pieces, part, me_ref, plan_ref, kept_ref, b_ref, *refs):
    a_refs, refs = refs[: len(arrivals)], refs[len(arrivals) :]
    before, refs = (refs[:2], refs[2:]) if which == FINAL else ((), refs)
    out_refs, (raw, halves, total, ring, a_sems, b_sems) = refs[:-6], refs[-6:]
    blocks = (halves.shape[0] - 1) // line
    count, piece, width = out_refs[0].shape[1:]
    rows = pieces * piece
    group, j = pl.program_id(0), pl.program_id(1)
    size = blocks * count * rows
    columns = out_refs[0].shape[0]
    q = me_ref[1] // 2
    begun = which * listed(blocks, count)
    ends = which * 2 * blocks
    end = kept_ref[FIELDS * (ends + 2 * blocks - 1)]

    def fetch(n):
        tile = plan_ref[FIELDS * n]
        slot = n % RING
        return pltpu.make_async_copy(b_ref.at[tile], ring.at[slot], b_sems.at[slot])

    @pl.when((group == 0) & (j == 0))
    def _():
        def each(act):
            for n, i in enumerate(arrivals):
                steps, link = (i + 1) // 2, (i + 1) % 2
                source = q if i == 0 else jnp.where(q % 2 == link, q + steps, q - steps)

                @pl.when((source >= 0) & (source < line))
                def _():
                    rows_of = a_refs[n].at[part * size : (part + 1) * size]
                    to = raw.at[pl.ds(pl.multiple_of(source * size, size), size)]
                    act(pltpu.make_async_copy(rows_of, to, a_sems.at[n]), source)

        each(lambda copy, _: copy.start())

        def begin(n, _):
            fetch(n).start()
            return 0

        lax.fori_loop(begun, jnp.minimum(end, begun + RING), begin, 0)
        halves[line * blocks] = jnp.zeros(halves.shape[1:], halves.dtype)

        def convert(i, _):
            first = pl.multiple_of(i * count * rows, count * rows)
            high, low = split(raw[pl.ds(first, count * rows)])
            halves[i, 0 : count * rows] = high
            halves[i, count * rows :] = low
            return 0

        def use(copy, source):
            copy.wait()
            lax.fori_loop(source * blocks, (source + 1) * blocks, convert, 0)

        each(use)

    def multiply(n):
        a = halves[plan_ref[FIELDS * n + 1]]
        slot = n % RING
        b_high, b_low = ring[slot, 0], ring[slot, 1]
        dot = functools.partial(jnp.dot, preferred_element_type=jnp.float32)
        by_high = dot(a, b_high)
        return by_high[: count * rows] + by_high[count * rows :] + dot(a[: count * rows], b_low)

    def step(first, i):
        n = first + 2 * i
        fetch(n).wait()
        fetch(n + 1).wait()
        products = [multiply(n), multiply(n + 1)]
        for e in range(2):
            levels = plan_ref[FIELDS * (n + e) + 2]
            for y in range(count):
                level = (levels >> (4 * y)) & 15
                total[level] += products[e][y * rows : (y + 1) * rows]

        @pl.when(n + RING < end)
        def _():
            fetch(n + RING).start()
            fetch(n + RING + 1).start()

        return first

    for u in range(columns):
        row = group * blocks + j * columns + u
        first = jnp.where(row == 0, begun, kept_ref[FIELDS * (ends + jnp.maximum(row - 1, 0))])
        total[...] = jnp.zeros_like(total)
        lax.fori_loop(
            0,
            (kept_ref[FIELDS * (ends + row)] - first) // 2,
            lambda i, first: step(first, i),
            first,
        )
        for g in range(2):

            @pl.when(group == g)
            def _():
                for m in range(count):
                    level = kept_ref[FIELDS * row + 1 + m]
                    for n in range(pieces):
                        some = pl.ds(n * piece, piece)
                        result = total[level, some]
                        if before:
                            result += before[g][u, m, some]
                        out_refs[g * pieces + n][u, m] = result


def product(me, plan, panel, parts, line, part, rows, which=ALL, before=(), pieces=1):
    blocks, count, width = panel.shape[1], panel.shape[3], panel.shape[6]
    arrivals = list(range(2 * line - 2))
    arrivals = {ALL: arrivals, EARLY: arrivals[:-1], FINAL: arrivals[-1:]}[which]
    out = jax.ShapeDtypeStruct((blocks, count, rows // pieces, width), jnp.float32)
    smem = pl.BlockSpec(memory_space=pltpu.SMEM)

    columns = min(COLUMNS, blocks)
    steps = blocks // columns

    def tiles_of(group, size):
        return pl.BlockSpec(
            (columns, count, size, width),
            lambda g, j: (jnp.where(g == group, j, 0 if group else steps - 1), 0, 0, 0),
        )

    return pl.pallas_call(
        functools.partial(product_kernel, line, which, arrivals, pieces, part),
        grid=(2, steps),
        out_shape=(out,) * (2 * pieces),
        in_specs=[smem] * 3
        + [pl.BlockSpec(memory_space=pl.ANY)] * (1 + len(arrivals))
        + [tiles_of(g, rows) for g in range(len(before))],
        out_specs=tuple(tiles_of(g, rows // pieces) for g in range(2) for _ in range(pieces)),
        scratch_shapes=[
            pltpu.VMEM((line * blocks * count * rows, width), jnp.float32),
            pltpu.VMEM((line * blocks + 1, 2 * count * rows, width), jnp.bfloat16),
            pltpu.VMEM((TR, rows, width), jnp.float32),
            pltpu.VMEM((RING, 2, width, width), jnp.bfloat16),
            pltpu.SemaphoreType.DMA((len(arrivals),)),
            pltpu.SemaphoreType.DMA((RING,)),
        ],
        compiler_params=pltpu.CompilerParams(vmem_limit_bytes=VMEM),
        cost_estimate=pl.CostEstimate(
            flops=3 * 32 * blocks * count * rows * width * width * len(arrivals) // (2 * line - 2),
            bytes_accessed=panel.size * len(arrivals) // (2 * line - 2),
            transcendentals=0,
        ),
        name="product",
    )(me, *plan, panel.reshape(-1, 2, width, width), *(parts[i] for i in arrivals), *before)


def inflate_kernel(own_ref, other_ref, out_ref):
    blocks, count, rows, width = own_ref.shape
    for j in range(blocks):
        partial = jnp.zeros((8, width), jnp.float32)
        for m in range(count):
            kept = own_ref[j, m] + other_ref[j, m]
            inflated = kept * kept
            out_ref[j, m * rows : (m + 1) * rows] = inflated
            for i in range(0, rows, 8):
                partial += inflated[i : i + 8]
        out_ref[j, count * rows :] = partial


def inflate(own, other):
    blocks, count, rows, width = own.shape
    return pl.pallas_call(
        inflate_kernel,
        out_shape=jax.ShapeDtypeStruct((blocks, count * rows + 8, width), jnp.float32),
        compiler_params=pltpu.CompilerParams(vmem_limit_bytes=VMEM),
        cost_estimate=pl.CostEstimate(
            flops=3 * own.size, bytes_accessed=12 * own.size, transcendentals=0
        ),
        name="inflate",
    )(own, other)


def owned_kernel(sizes, blocks, count, scale, me_ref, *refs):
    chunks = len(sizes)
    notes, refs = refs[:4], refs[4:]
    sources = refs[: 4 * chunks]
    out_ref, slots, partial, whose, in_sems, out_sems, sum_sems = refs[4 * chunks :]
    items = blocks * count
    most = items // 2
    r = me_ref[0]
    starts = [sum(sizes[:h]) for h in range(chunks)]

    def partials(act):
        for i in range(4 * chunks):
            rows = pl.ds(count * sizes[i // 4], 8)
            act(pltpu.make_async_copy(sources[i].at[:, rows], partial.at[i], sum_sems.at[i]))

    partials(lambda copy: copy.start())
    for s in range(4 * most):
        whose[s] = -1
    for relative in range(4):
        rr = jnp.bitwise_xor(r, relative)

        def place_item(f, n, relative=relative, rr=rr):
            mine = notes[relative][0, 2 * items + f].astype(jnp.int32) == r

            @pl.when(mine)
            def _():
                slot = rr * most + n
                whose[slot] = f // count
                for h in range(chunks):
                    pltpu.make_async_copy(
                        sources[4 * h + relative].at[
                            f // count, pl.ds(pl.multiple_of(f % count * sizes[h], 8), sizes[h])
                        ],
                        slots.at[slot, pl.ds(starts[h], sizes[h])],
                        in_sems.at[slot],
                    ).start()

            return n + mine.astype(jnp.int32)

        lax.fori_loop(0, items, place_item, jnp.int32(0))

    partials(lambda copy: copy.wait())
    totals = jnp.sum(jnp.sum(partial[...], axis=0), axis=1)

    def finish(s, _):
        j = whose[s]

        @pl.when(j < 0)
        def _():
            slots[s] = jnp.zeros(slots.shape[1:], jnp.float32)

        for jj in range(blocks):

            @pl.when(j == jj)
            def _():
                pltpu.make_async_copy(slots.at[s], slots.at[s], in_sems.at[s]).wait()
                slots[s] = scale * slots[s] / totals[jj : jj + 1]

        pltpu.make_async_copy(slots.at[s], out_ref.at[s], out_sems.at[s]).start()
        return 0

    lax.fori_loop(0, 4 * most, finish, 0)

    def drain(s, _):
        pltpu.make_async_copy(slots.at[s], out_ref.at[s], out_sems.at[s]).wait()
        return 0

    lax.fori_loop(0, 4 * most, drain, 0)


def owned_tiles(me, notes, sources, sizes, count, scale):
    blocks, _, width = sources[0].shape
    most = blocks * count // 2
    smem = pl.BlockSpec(memory_space=pltpu.SMEM)
    return pl.pallas_call(
        functools.partial(owned_kernel, sizes, blocks, count, scale),
        grid=(1,),
        out_shape=jax.ShapeDtypeStruct((4 * most, width, width), jnp.float32),
        in_specs=[smem, *(spec for _, spec in notes)]
        + [pl.BlockSpec(memory_space=pl.ANY)] * len(sources),
        out_specs=pl.BlockSpec(memory_space=pl.ANY),
        scratch_shapes=[
            pltpu.VMEM((4 * most, width, width), jnp.float32),
            pltpu.VMEM((len(sources), blocks, 8, width), jnp.float32),
            pltpu.SMEM((4 * most,), jnp.int32),
            pltpu.SemaphoreType.DMA((4 * most,)),
            pltpu.SemaphoreType.DMA((4 * most,)),
            pltpu.SemaphoreType.DMA((len(sources),)),
        ],
        compiler_params=pltpu.CompilerParams(vmem_limit_bytes=VMEM),
        cost_estimate=pl.CostEstimate(
            flops=4 * most * width * width,
            bytes_accessed=32 * most * width * width,
            transcendentals=0,
        ),
        name="owned",
    )(me, *(x for x, _ in notes), *sources)


def on_device(columns, matrix_tiles, tile_rows, keep_rows, owners):
    tiles = matrix_tiles[0]
    blocks, count, width = tiles.shape[0], tiles.shape[1], tiles.shape[2]
    line = columns // 2
    r, c = lax.axis_index("row"), lax.axis_index("col")
    me = jnp.stack([r, c]).astype(jnp.int32)

    core = functools.partial(lax.ppermute, axis_name="row", perm=[(i, i ^ 1) for i in range(4)])
    across = functools.partial(lax.ppermute, axis_name="row", perm=[(i, i ^ 2) for i in range(4)])
    pair = functools.partial(
        lax.ppermute, axis_name="col", perm=[(i, i ^ 1) for i in range(columns)]
    )

    links = []
    for first in (0, 1):
        perm = []
        for i in range(4 * columns):
            rank = i % columns // 2
            to = rank + 1 if rank % 2 == first else rank - 1
            inside = 0 <= to < line
            perm.append((i, i + 2 * (to - rank) if inside else i ^ columns))
        links.append(functools.partial(lax.ppermute, axis_name=("row", "col"), perm=perm))

    sizes = tuple(size * width // sum(CHUNKS) for size in CHUNKS)
    starts = [sum(sizes[:h]) for h in range(len(sizes))]

    chunks, half = len(sizes), width // 2
    rows = [size * width // sum(CHUNKS) for size in ROWS]

    def cut(x, h):
        x = x[:, :, starts[h] : starts[h] + sizes[h]]
        x = x.reshape(blocks * count, sizes[h] // rows[h], rows[h], width)
        return jnp.swapaxes(x, 0, 1).reshape(-1, width)

    notes = jnp.concatenate([tile_rows.reshape(-1), keep_rows.reshape(-1), owners.reshape(-1)])
    notes = jnp.pad(notes.astype(jnp.float32), (0, width - notes.shape[0]))
    own = [jnp.concatenate([cut(tiles, 0), jnp.broadcast_to(notes, (8, width))])]
    came = [[] for _ in sizes]

    ticks = {}

    def at(tick, x):
        ticks.setdefault(tick, []).append(x)
        return x

    def tie(x, *others):
        return lax.optimization_barrier((x, *others))[0] if others else x

    def after(tick, x):
        return tie(x, *ticks.get(tick - 1, ()))

    def send(tick, move, x, *more):
        return at(tick, move(after(tick, x), *more))

    def swap(tick, x, *others):
        return at(tick + 1, core(after(tick, tie(x, *others))))

    base = line - 1
    hops = {}
    for h in range(chunks):
        for hop in range(line - 1):
            if h == 0:
                tick = hop
            else:
                tick = base + hop + (h - 1 if hop else max(h - 2, 0))
            hops.setdefault(tick, []).append((h, hop))

    panel = None
    sources, waiting, landed, flying = [], [], [], []
    begun, made, cuts = {}, [], CUTS

    def put(tick, group, relative, *parts):
        nonlocal panel
        panel, mark = place(parts, panel, group, relative, blocks, count)
        at(tick, mark)

    items = blocks * count
    upper, parts = sizes[0] * items, sizes[0] // rows[0]

    def halves(top, low, number=0):
        upper_rows = ((top, rows[0], part * items) for part in range(parts))
        return (*upper_rows, (low, half, number * items))

    tick = 0
    while tick <= max(hops) + 1 or landed or flying:
        for h in range(1, chunks):
            if (h, line - 2) in hops.get(tick - 1, ()):
                results = product(
                    me, plan, panel, [own[h], *came[h]], line, 0, rows[h], FINAL, begun[h], cuts[h]
                )
                at(tick - 1, results[0])
                made.append((results[: cuts[h]], results[cuts[h] :]))
        for h, hop in hops.get(tick, ()):
            if hop:
                operands = came[h][-1], came[h][-2]
            else:
                operands = own[h], own[h]
            for link in range(1 if hop == line - 2 else 2):
                came[h].append(send(tick, links[link], operands[link]))
            if h and hop == line - 2:
                begun[h] = product(
                    me, plan, panel, [own[h], *came[h][:-1]], line, 0, rows[h], EARLY
                )
                at(tick, begun[h][0])
        if tick == 0:
            whole = tiles.reshape(-1, width)
            rest = tie(tiles, own[0])[:, :, half:].reshape(-1, width)
            b_pair, b_across = send(0, pair, own[0]), send(0, across, own[0])
            core_own = swap(0, whole)
            put(0, 1, 0, *halves(own[0], rest))
        if tick == 1:
            pair_rest, across_rest = send(1, pair, rest), send(1, across, rest)
            core_pair = at(1, swap(1, b_pair))
            put(1, 1, 1, (core_own, width, 0))
            later = after(1, tiles)
            own += [at(1, cut(later, h)) for h in range(1, chunks)]
        if tick == 2:
            diagonal, diagonal_rest = send(2, across, b_pair), send(2, pair, across_rest)
            core_across = swap(2, b_across)
            core_rest = swap(2, jnp.concatenate([pair_rest, across_rest, own[0][upper:]]))
            put(2, 0, 0, *halves(b_pair, pair_rest))
            put(2, 1, 2, *halves(b_across, across_rest))
            put(2, 0, 1, *halves(core_pair, core_rest))
            put(2, 1, 3, *halves(core_across, core_rest, 1))
        if tick == max(base, 3):
            core_diagonal = swap(tick, diagonal)
            put(tick, 0, 2, *halves(diagonal, diagonal_rest))
            core_diagonal_rest = swap(tick, diagonal_rest, core_diagonal)
            put(tick, 0, 3, *halves(core_diagonal, core_diagonal_rest))
            known = [
                (b_pair, upper),
                (own[0], upper),
                (core_pair, upper),
                (core_rest, 2 * half * items),
                (diagonal, upper),
                (b_across, upper),
                (core_diagonal, upper),
                (core_across, upper),
            ]
            known = [noted(x, i) for x, i in known]
            shards = [noted(x, upper) for x in [own[0], *came[0]]]
            plan = make_plan(me, known, shards, line, blocks, count)
            gathered = [own[0], *came[0]]
            waiting = [(gathered, i, rows[0]) for i in range(parts)]
        if flying and flying[0][0] < tick:
            _, mine, other = flying.pop(0)
            inflated = inflate(mine, other)
            opposite = send(tick, across, inflated)
            sources += [inflated, core(inflated), opposite, core(opposite)]
        if landed and landed[0][0] < tick:
            _, theirs, mine = landed.pop(0)
            other = send(tick, pair, theirs)
            flying.append((tick, mine, other))
        if waiting:
            gathered, part, size = waiting.pop(0)
            theirs, mine = product(me, plan, panel, gathered, line, part, size)
            landed.append((tick, at(tick, theirs), mine))
        tick += 1
    for theirs, mine in made:
        others = [pair(tie(x, other)) for x in theirs]
        other = others[-1]
        inflated = []
        for x, y in zip(mine, others):
            inflated.append(inflate(x, tie(y, *inflated[-1:])))
        for x in inflated:
            opposite = across(tie(x, opposite))
            sources += [x, core(x), opposite, core(opposite)]
    sizes = tuple(
        rows[h] // cuts[h]
        for h in range(chunks)
        for _ in range(0, sizes[h], rows[h] // cuts[h])
    )
    scale = float(4 * TR * width)
    owned = owned_tiles(me, known[1::2], sources, sizes, count, scale)
    return owned[None, None]


def solution(mesh):
    placed = (
        P("row", "col", None, None, None),
        P("row", "col", None),
        P("row", "col", None),
        P("row", "col", None),
    )
    return jax.shard_map(
        functools.partial(on_device, mesh.shape["col"]),
        mesh=mesh,
        in_specs=placed,
        out_specs=P("row", "col", None, None, None),
        check_vma=False,
    )
```

```python
import functools

import jax
import jax.numpy as jnp
from jax import lax
from jax.experimental import pallas as pl
from jax.experimental.pallas import tpu as pltpu
from jax.sharding import PartitionSpec as P

TR = 8
CHUNKS = (128, 64, 64)
ROWS = (64, 64, 64)
CUTS = (1, 1, 1)
FIELDS = 8
ALL, EARLY, FINAL = 0, 1, 2
RING = 16
COLUMNS = 2
VMEM = 56 * 1024 * 1024


def arrival(q, source):
    steps = jnp.abs(source - q)
    link = (q + (source < q)) % 2
    return jnp.where(steps == 0, 0, 2 * steps - 1 + link)


def split(x):
    high = x.astype(jnp.bfloat16)
    low = (x - high.astype(jnp.float32)).astype(jnp.bfloat16)
    return high, low


def place_kernel(parts, *refs):
    o_ref, mark_ref = refs[-2:]
    mark_ref[...] = jnp.zeros_like(mark_ref)
    count = o_ref.shape[3]
    start = 0
    for x_ref in refs[:parts]:
        rows = x_ref.shape[0] // count
        for z in range(count):
            high, low = split(x_ref[z * rows : (z + 1) * rows])
            o_ref[0, 0, 0, z, 0, start : start + rows] = high
            o_ref[0, 0, 0, z, 1, start : start + rows] = low
        start += rows


def place(parts, buffer, group, relative, blocks, count):
    width = parts[0][0].shape[1]
    out = jax.ShapeDtypeStruct((2, blocks, 4, count, 2, width, width), jnp.bfloat16)
    in_specs = [
        pl.BlockSpec((count * rows, width), lambda j, first=first: (first // count + j, 0))
        for _, rows, first in parts
    ]
    args = [x for x, _, _ in parts]
    aliases = {}
    if buffer is not None:
        in_specs.append(pl.BlockSpec(memory_space=pl.ANY))
        args.append(buffer)
        aliases = {len(parts): 0}
    size = blocks * count * width * width
    return pl.pallas_call(
        functools.partial(place_kernel, len(parts)),
        grid=(blocks,),
        out_shape=(out, jax.ShapeDtypeStruct((8, 128), jnp.float32)),
        in_specs=in_specs,
        out_specs=(
            pl.BlockSpec(
                (1, 1, 1, count, 2, width, width), lambda j: (group, j, relative, 0, 0, 0, 0)
            ),
            pl.BlockSpec((8, 128), lambda j: (0, 0)),
        ),
        input_output_aliases=aliases,
        compiler_params=pltpu.CompilerParams(vmem_limit_bytes=VMEM),
        cost_estimate=pl.CostEstimate(flops=size, bytes_accessed=8 * size, transcendentals=0),
        name="place",
    )(*args)


def join_kernel(firsts, *refs):
    out_ref, sems = refs[-2:]
    start, copies = 0, []
    for i, (first, x_ref) in enumerate(zip(firsts, refs)):
        rows = x_ref.shape[0] - first
        to = out_ref.at[start : start + rows]
        copies.append(pltpu.make_async_copy(x_ref.at[first : first + rows], to, sems.at[i]))
        start += rows
    for copy in copies:
        copy.start()
    for copy in copies:
        copy.wait()


def join(*parts):
    arrays, firsts = zip(*parts)
    rows = sum(x.shape[0] - first for x, first in parts)
    return pl.pallas_call(
        functools.partial(join_kernel, firsts),
        out_shape=jax.ShapeDtypeStruct((rows, arrays[0].shape[1]), arrays[0].dtype),
        in_specs=[pl.BlockSpec(memory_space=pl.ANY)] * len(parts),
        out_specs=pl.BlockSpec(memory_space=pl.ANY),
        scratch_shapes=[pltpu.SemaphoreType.DMA((len(parts),))],
        compiler_params=pltpu.CompilerParams(vmem_limit_bytes=VMEM),
        cost_estimate=pl.CostEstimate(
            flops=0, bytes_accessed=8 * rows * arrays[0].shape[1], transcendentals=0
        ),
        name="join",
    )(*arrays)


def plan_kernel(line, blocks, count, me_ref, *refs):
    items = blocks * count
    room = listed(blocks, count)
    known, shards = refs[:8], refs[8:-3]
    plan_ref, kept_ref, levels_ref = refs[-3:]
    r, c = me_ref[0], me_ref[1]
    q, p = c // 2, c % 2

    for i, shard in enumerate(shards):

        def note(j, _, i=i, shard=shard):
            levels = jnp.int32(0)
            for y in range(count):
                levels += shard[0, j * count + y].astype(jnp.int32) << (4 * y)
            levels_ref[i * blocks + j] = levels
            return 0

        lax.fori_loop(0, blocks, note, 0)

    def write(n, tile, at, levels):
        plan_ref[FIELDS * n] = tile
        plan_ref[FIELDS * n + 1] = at
        plan_ref[FIELDS * n + 2] = levels

    ends = tuple(jnp.int32(i * room) for i in range(3))
    for group in range(2):

        def column(j, ends, group=group):
            row = group * blocks + j
            for relative in range(4):
                rr = jnp.bitwise_xor(r, relative)

                def entry(z, ends, relative=relative, rr=rr):
                    noted = known[2 * relative + group][0, j * count + z]
                    k = rr * TR + noted.astype(jnp.int32)
                    ck = k // blocks
                    mine = ck % 2 == p
                    came = jnp.where(mine, arrival(q, ck // 2), 0)
                    final = came == 2 * line - 3
                    tile = (row * 4 + relative) * count + z
                    at = (ck // 2) * blocks + k % blocks
                    levels = levels_ref[came * blocks + k % blocks]
                    write(ends[0], tile, at, levels)
                    write(jnp.where(final, ends[2], ends[1]), tile, at, levels)
                    return (
                        ends[0] + mine.astype(jnp.int32),
                        ends[1] + (mine & ~final).astype(jnp.int32),
                        ends[2] + (mine & final).astype(jnp.int32),
                    )

                ends = lax.fori_loop(0, count, entry, ends)
            filled = []
            for i, n in enumerate(ends):
                write(n, row * 4 * count, line * blocks, jnp.int32(0))
                filled.append(n + n % 2)
                kept_ref[FIELDS * (i * 2 * blocks + row)] = filled[-1]
            for m in range(count):
                noted = known[group][0, items + j * count + m]
                kept_ref[FIELDS * row + 1 + m] = noted.astype(jnp.int32)
            return tuple(filled)

        ends = lax.fori_loop(0, blocks, column, ends)


def listed(blocks, count):
    return 2 * blocks * (4 * count + 1) + 2


def noted(x, row):
    return x, pl.BlockSpec((8, 128), lambda *_: (row // 8, 0), memory_space=pltpu.SMEM)


def make_plan(me, known, shards, line, blocks, count):
    smem = pl.BlockSpec(memory_space=pltpu.SMEM)
    args, specs = zip(*known, *shards)
    return pl.pallas_call(
        functools.partial(plan_kernel, line, blocks, count),
        grid=(1,),
        out_shape=(
            jax.ShapeDtypeStruct((3 * FIELDS * listed(blocks, count),), jnp.int32),
            jax.ShapeDtypeStruct((3 * FIELDS * 2 * blocks,), jnp.int32),
        ),
        in_specs=[smem, *specs],
        out_specs=(smem, smem),
        scratch_shapes=[pltpu.SMEM(((2 * line - 2) * blocks,), jnp.int32)],
        name="plan",
    )(me, *args)


def product_kernel(line, which, arrivals, pieces, part, me_ref, plan_ref, kept_ref, b_ref, *refs):
    a_refs, refs = refs[: len(arrivals)], refs[len(arrivals) :]
    before, refs = (refs[:2], refs[2:]) if which == FINAL else ((), refs)
    out_refs, (raw, halves, total, ring, a_sems, b_sems) = refs[:-6], refs[-6:]
    blocks = (halves.shape[0] - 1) // line
    count, piece, width = out_refs[0].shape[1:]
    rows = pieces * piece
    group, j = pl.program_id(0), pl.program_id(1)
    size = blocks * count * rows
    columns = out_refs[0].shape[0]
    q = me_ref[1] // 2
    begun = which * listed(blocks, count)
    ends = which * 2 * blocks
    end = kept_ref[FIELDS * (ends + 2 * blocks - 1)]

    def fetch(n):
        tile = plan_ref[FIELDS * n]
        slot = n % RING
        return pltpu.make_async_copy(b_ref.at[tile], ring.at[slot], b_sems.at[slot])

    @pl.when((group == 0) & (j == 0))
    def _():
        def each(act):
            for n, i in enumerate(arrivals):
                steps, link = (i + 1) // 2, (i + 1) % 2
                source = q if i == 0 else jnp.where(q % 2 == link, q + steps, q - steps)

                @pl.when((source >= 0) & (source < line))
                def _():
                    rows_of = a_refs[n].at[part * size : (part + 1) * size]
                    to = raw.at[pl.ds(pl.multiple_of(source * size, size), size)]
                    act(pltpu.make_async_copy(rows_of, to, a_sems.at[n]), source)

        each(lambda copy, _: copy.start())

        def begin(n, _):
            fetch(n).start()
            return 0

        lax.fori_loop(begun, jnp.minimum(end, begun + RING), begin, 0)
        halves[line * blocks] = jnp.zeros(halves.shape[1:], halves.dtype)

        def convert(i, _):
            first = pl.multiple_of(i * count * rows, count * rows)
            high, low = split(raw[pl.ds(first, count * rows)])
            halves[i, 0 : count * rows] = high
            halves[i, count * rows :] = low
            return 0

        def use(copy, source):
            copy.wait()
            lax.fori_loop(source * blocks, (source + 1) * blocks, convert, 0)

        each(use)

    def multiply(n):
        a = halves[plan_ref[FIELDS * n + 1]]
        slot = n % RING
        b_high, b_low = ring[slot, 0], ring[slot, 1]
        dot = functools.partial(jnp.dot, preferred_element_type=jnp.float32)
        by_high = dot(a, b_high)
        return by_high[: count * rows] + by_high[count * rows :] + dot(a[: count * rows], b_low)

    def step(first, i):
        n = first + 2 * i
        fetch(n).wait()
        fetch(n + 1).wait()
        products = [multiply(n), multiply(n + 1)]
        for e in range(2):
            levels = plan_ref[FIELDS * (n + e) + 2]
            for y in range(count):
                level = (levels >> (4 * y)) & 15
                total[level] += products[e][y * rows : (y + 1) * rows]

        @pl.when(n + RING < end)
        def _():
            fetch(n + RING).start()
            fetch(n + RING + 1).start()

        return first

    for u in range(columns):
        row = group * blocks + j * columns + u
        first = jnp.where(row == 0, begun, kept_ref[FIELDS * (ends + jnp.maximum(row - 1, 0))])
        total[...] = jnp.zeros_like(total)
        lax.fori_loop(
            0,
            (kept_ref[FIELDS * (ends + row)] - first) // 2,
            lambda i, first: step(first, i),
            first,
        )
        for g in range(2):

            @pl.when(group == g)
            def _():
                for m in range(count):
                    level = kept_ref[FIELDS * row + 1 + m]
                    for n in range(pieces):
                        some = pl.ds(n * piece, piece)
                        result = total[level, some]
                        if before:
                            result += before[g][u, m, some]
                        out_refs[g * pieces + n][u, m] = result


def product(me, plan, panel, parts, line, part, rows, which=ALL, before=(), pieces=1):
    blocks, count, width = panel.shape[1], panel.shape[3], panel.shape[6]
    arrivals = list(range(2 * line - 2))
    arrivals = {ALL: arrivals, EARLY: arrivals[:-1], FINAL: arrivals[-1:]}[which]
    out = jax.ShapeDtypeStruct((blocks, count, rows // pieces, width), jnp.float32)
    smem = pl.BlockSpec(memory_space=pltpu.SMEM)

    columns = min(COLUMNS, blocks)
    steps = blocks // columns

    def tiles_of(group, size):
        return pl.BlockSpec(
            (columns, count, size, width),
            lambda g, j: (jnp.where(g == group, j, 0 if group else steps - 1), 0, 0, 0),
        )

    return pl.pallas_call(
        functools.partial(product_kernel, line, which, arrivals, pieces, part),
        grid=(2, steps),
        out_shape=(out,) * (2 * pieces),
        in_specs=[smem] * 3
        + [pl.BlockSpec(memory_space=pl.ANY)] * (1 + len(arrivals))
        + [tiles_of(g, rows) for g in range(len(before))],
        out_specs=tuple(tiles_of(g, rows // pieces) for g in range(2) for _ in range(pieces)),
        scratch_shapes=[
            pltpu.VMEM((line * blocks * count * rows, width), jnp.float32),
            pltpu.VMEM((line * blocks + 1, 2 * count * rows, width), jnp.bfloat16),
            pltpu.VMEM((TR, rows, width), jnp.float32),
            pltpu.VMEM((RING, 2, width, width), jnp.bfloat16),
            pltpu.SemaphoreType.DMA((len(arrivals),)),
            pltpu.SemaphoreType.DMA((RING,)),
        ],
        compiler_params=pltpu.CompilerParams(vmem_limit_bytes=VMEM),
        cost_estimate=pl.CostEstimate(
            flops=3 * 32 * blocks * count * rows * width * width * len(arrivals) // (2 * line - 2),
            bytes_accessed=panel.size * len(arrivals) // (2 * line - 2),
            transcendentals=0,
        ),
        name="product",
    )(me, *plan, panel.reshape(-1, 2, width, width), *(parts[i] for i in arrivals), *before)


def inflate_kernel(own_ref, other_ref, out_ref):
    blocks, count, rows, width = own_ref.shape
    for j in range(blocks):
        partial = jnp.zeros((8, width), jnp.float32)
        for m in range(count):
            kept = own_ref[j, m] + other_ref[j, m]
            inflated = kept * kept
            out_ref[j, m * rows : (m + 1) * rows] = inflated
            for i in range(0, rows, 8):
                partial += inflated[i : i + 8]
        out_ref[j, count * rows :] = partial


def inflate(own, other):
    blocks, count, rows, width = own.shape
    return pl.pallas_call(
        inflate_kernel,
        out_shape=jax.ShapeDtypeStruct((blocks, count * rows + 8, width), jnp.float32),
        compiler_params=pltpu.CompilerParams(vmem_limit_bytes=VMEM),
        cost_estimate=pl.CostEstimate(
            flops=3 * own.size, bytes_accessed=12 * own.size, transcendentals=0
        ),
        name="inflate",
    )(own, other)


def owned_kernel(sizes, blocks, count, scale, me_ref, *refs):
    chunks = len(sizes)
    notes, refs = refs[:4], refs[4:]
    sources = refs[: 4 * chunks]
    out_ref, slots, partial, whose, in_sems, out_sems, sum_sems = refs[4 * chunks :]
    items = blocks * count
    most = items // 2
    r = me_ref[0]
    starts = [sum(sizes[:h]) for h in range(chunks)]

    def partials(act):
        for i in range(4 * chunks):
            rows = pl.ds(count * sizes[i // 4], 8)
            act(pltpu.make_async_copy(sources[i].at[:, rows], partial.at[i], sum_sems.at[i]))

    partials(lambda copy: copy.start())
    for s in range(4 * most):
        whose[s] = -1
    for relative in range(4):
        rr = jnp.bitwise_xor(r, relative)

        def place_item(f, n, relative=relative, rr=rr):
            mine = notes[relative][0, 2 * items + f].astype(jnp.int32) == r

            @pl.when(mine)
            def _():
                slot = rr * most + n
                whose[slot] = f // count
                for h in range(chunks):
                    pltpu.make_async_copy(
                        sources[4 * h + relative].at[
                            f // count, pl.ds(pl.multiple_of(f % count * sizes[h], 8), sizes[h])
                        ],
                        slots.at[slot, pl.ds(starts[h], sizes[h])],
                        in_sems.at[slot],
                    ).start()

            return n + mine.astype(jnp.int32)

        lax.fori_loop(0, items, place_item, jnp.int32(0))

    partials(lambda copy: copy.wait())
    totals = jnp.sum(jnp.sum(partial[...], axis=0), axis=1)

    def finish(s, _):
        j = whose[s]

        @pl.when(j < 0)
        def _():
            slots[s] = jnp.zeros(slots.shape[1:], jnp.float32)

        for jj in range(blocks):

            @pl.when(j == jj)
            def _():
                pltpu.make_async_copy(slots.at[s], slots.at[s], in_sems.at[s]).wait()
                slots[s] = scale * slots[s] / totals[jj : jj + 1]

        pltpu.make_async_copy(slots.at[s], out_ref.at[s], out_sems.at[s]).start()
        return 0

    lax.fori_loop(0, 4 * most, finish, 0)

    def drain(s, _):
        pltpu.make_async_copy(slots.at[s], out_ref.at[s], out_sems.at[s]).wait()
        return 0

    lax.fori_loop(0, 4 * most, drain, 0)


def owned_tiles(me, notes, sources, sizes, count, scale):
    blocks, _, width = sources[0].shape
    most = blocks * count // 2
    smem = pl.BlockSpec(memory_space=pltpu.SMEM)
    return pl.pallas_call(
        functools.partial(owned_kernel, sizes, blocks, count, scale),
        grid=(1,),
        out_shape=jax.ShapeDtypeStruct((4 * most, width, width), jnp.float32),
        in_specs=[smem, *(spec for _, spec in notes)]
        + [pl.BlockSpec(memory_space=pl.ANY)] * len(sources),
        out_specs=pl.BlockSpec(memory_space=pl.ANY),
        scratch_shapes=[
            pltpu.VMEM((4 * most, width, width), jnp.float32),
            pltpu.VMEM((len(sources), blocks, 8, width), jnp.float32),
            pltpu.SMEM((4 * most,), jnp.int32),
            pltpu.SemaphoreType.DMA((4 * most,)),
            pltpu.SemaphoreType.DMA((4 * most,)),
            pltpu.SemaphoreType.DMA((len(sources),)),
        ],
        compiler_params=pltpu.CompilerParams(vmem_limit_bytes=VMEM),
        cost_estimate=pl.CostEstimate(
            flops=4 * most * width * width,
            bytes_accessed=32 * most * width * width,
            transcendentals=0,
        ),
        name="owned",
    )(me, *(x for x, _ in notes), *sources)


def on_device(columns, matrix_tiles, tile_rows, keep_rows, owners):
    tiles = matrix_tiles[0]
    blocks, count, width = tiles.shape[0], tiles.shape[1], tiles.shape[2]
    line = columns // 2
    r, c = lax.axis_index("row"), lax.axis_index("col")
    me = jnp.stack([r, c]).astype(jnp.int32)

    core = functools.partial(lax.ppermute, axis_name="row", perm=[(i, i ^ 1) for i in range(4)])
    across = functools.partial(lax.ppermute, axis_name="row", perm=[(i, i ^ 2) for i in range(4)])
    pair = functools.partial(
        lax.ppermute, axis_name="col", perm=[(i, i ^ 1) for i in range(columns)]
    )

    links = []
    for first in (0, 1):
        perm = []
        for i in range(4 * columns):
            rank = i % columns // 2
            to = rank + 1 if rank % 2 == first else rank - 1
            inside = 0 <= to < line
            perm.append((i, i + 2 * (to - rank) if inside else i ^ columns))
        links.append(functools.partial(lax.ppermute, axis_name=("row", "col"), perm=perm))

    sizes = tuple(size * width // sum(CHUNKS) for size in CHUNKS)
    starts = [sum(sizes[:h]) for h in range(len(sizes))]

    chunks, half = len(sizes), width // 2
    rows = [size * width // sum(CHUNKS) for size in ROWS]

    def cut(x, h):
        x = x[:, :, starts[h] : starts[h] + sizes[h]]
        x = x.reshape(blocks * count, sizes[h] // rows[h], rows[h], width)
        return jnp.swapaxes(x, 0, 1).reshape(-1, width)

    notes = jnp.concatenate([tile_rows.reshape(-1), keep_rows.reshape(-1), owners.reshape(-1)])
    notes = jnp.pad(notes.astype(jnp.float32), (0, width - notes.shape[0]))
    own = [jnp.concatenate([cut(tiles, 0), jnp.broadcast_to(notes, (8, width))])]
    came = [[] for _ in sizes]

    ticks = {}

    def at(tick, x):
        ticks.setdefault(tick, []).append(x)
        return x

    def tie(x, *others):
        return lax.optimization_barrier((x, *others))[0] if others else x

    def after(tick, x):
        return tie(x, *ticks.get(tick - 1, ()))

    def send(tick, move, x, *more):
        return at(tick, move(after(tick, x), *more))

    def swap(tick, x, *others):
        return at(tick + 1, core(after(tick, tie(x, *others))))

    base = line - 1
    hops = {}
    for h in range(chunks):
        for hop in range(line - 1):
            if h == 0:
                tick = hop
            else:
                tick = base + hop + (h - 1 if hop else max(h - 2, 0))
            hops.setdefault(tick, []).append((h, hop))

    panel = None
    sources, waiting, landed, flying = [], [], [], []
    begun, made, cuts = {}, [], CUTS

    def put(tick, group, relative, *parts):
        nonlocal panel
        panel, mark = place(parts, panel, group, relative, blocks, count)
        at(tick, mark)

    items = blocks * count
    upper, parts = sizes[0] * items, sizes[0] // rows[0]

    def halves(top, low, number=0):
        upper_rows = ((top, rows[0], part * items) for part in range(parts))
        return (*upper_rows, (low, half, number * items))

    tick = 0
    while tick <= max(hops) + 1 or landed or flying:
        for h in range(1, chunks):
            if (h, line - 2) in hops.get(tick - 1, ()):
                results = product(
                    me, plan, panel, [own[h], *came[h]], line, 0, rows[h], FINAL, begun[h], cuts[h]
                )
                at(tick - 1, results[0])
                made.append((results[: cuts[h]], results[cuts[h] :]))
        for h, hop in hops.get(tick, ()):
            if hop:
                operands = came[h][-1], came[h][-2]
            else:
                operands = own[h], own[h]
            for link in range(1 if hop == line - 2 else 2):
                came[h].append(send(tick, links[link], operands[link]))
            if h and hop == line - 2:
                begun[h] = product(
                    me, plan, panel, [own[h], *came[h][:-1]], line, 0, rows[h], EARLY
                )
                at(tick, begun[h][0])
        if tick == 0:
            whole = tiles.reshape(-1, width)
            rest = tie(tiles, own[0])[:, :, half:].reshape(-1, width)
            b_pair, b_across = send(0, pair, own[0]), send(0, across, own[0])
            core_own = swap(0, whole)
            put(0, 1, 0, *halves(own[0], rest))
        if tick == 1:
            pair_rest, across_rest = send(1, pair, rest), send(1, across, rest)
            core_pair = at(1, swap(1, b_pair))
            put(1, 1, 1, (core_own, width, 0))
            later = after(1, tiles)
            own += [at(1, cut(later, h)) for h in range(1, chunks)]
        if tick == 2:
            diagonal, diagonal_rest = send(2, across, b_pair), send(2, pair, across_rest)
            core_across = swap(2, b_across)
            core_rest = swap(2, join((pair_rest, 0), (across_rest, 0), (own[0], upper)))
            put(2, 0, 0, *halves(b_pair, pair_rest))
            put(2, 1, 2, *halves(b_across, across_rest))
            put(2, 0, 1, *halves(core_pair, core_rest))
            put(2, 1, 3, *halves(core_across, core_rest, 1))
        if tick == max(base, 3):
            core_diagonal = swap(tick, diagonal)
            put(tick, 0, 2, *halves(diagonal, diagonal_rest))
            core_diagonal_rest = swap(tick, diagonal_rest, core_diagonal)
            put(tick, 0, 3, *halves(core_diagonal, core_diagonal_rest))
            known = [
                (b_pair, upper),
                (own[0], upper),
                (core_pair, upper),
                (core_rest, 2 * half * items),
                (diagonal, upper),
                (b_across, upper),
                (core_diagonal, upper),
                (core_across, upper),
            ]
            known = [noted(x, i) for x, i in known]
            shards = [noted(x, upper) for x in [own[0], *came[0]]]
            plan = make_plan(me, known, shards, line, blocks, count)
            gathered = [own[0], *came[0]]
            waiting = [(gathered, i, rows[0]) for i in range(parts)]
        if flying and flying[0][0] < tick:
            _, mine, other = flying.pop(0)
            inflated = inflate(mine, other)
            opposite = send(tick, across, inflated)
            sources += [inflated, core(inflated), opposite, core(opposite)]
        if landed and landed[0][0] < tick:
            _, theirs, mine = landed.pop(0)
            other = send(tick, pair, theirs)
            flying.append((tick, mine, other))
        if waiting:
            gathered, part, size = waiting.pop(0)
            theirs, mine = product(me, plan, panel, gathered, line, part, size)
            landed.append((tick, at(tick, theirs), mine))
        tick += 1
    for theirs, mine in made:
        others = [pair(tie(x, other)) for x in theirs]
        other = others[-1]
        inflated = []
        for x, y in zip(mine, others):
            inflated.append(inflate(x, tie(y, *inflated[-1:])))
        for x in inflated:
            opposite = across(tie(x, opposite))
            sources += [x, core(x), opposite, core(opposite)]
    sizes = tuple(
        rows[h] // cuts[h]
        for h in range(chunks)
        for _ in range(0, sizes[h], rows[h] // cuts[h])
    )
    scale = float(4 * TR * width)
    owned = owned_tiles(me, known[1::2], sources, sizes, count, scale)
    return owned[None, None]


def solution(mesh):
    placed = (
        P("row", "col", None, None, None),
        P("row", "col", None),
        P("row", "col", None),
        P("row", "col", None),
    )
    return jax.shard_map(
        functools.partial(on_device, mesh.shape["col"]),
        mesh=mesh,
        in_specs=placed,
        out_specs=P("row", "col", None, None, None),
        check_vma=False,
    )
```
